256 devices in a mesh: band: 32 (over z_hi, x, core), grid: 8 (over y, z_lo).
Axes of the slice: x: 4, y: 4, z: 8 (z_hi: 4, z_lo: 2; z = z_hi * 2 + z_lo), core: 2. Of those that a mesh axis runs over, the one named last changes fastest.
Arguments:
- orbitals: float32 [64, 72, 5184], P('band', 'grid'), may hold values from -4 to 4
- block_owner: int32 [2], replicated, may hold values from 0 to 31
Outputs:
- exchange_field: float32 [64, 72, 5184], P('band', 'grid')
- block_field: float32 [2, 2, 72, 5184], P(None, None, 'grid', 'band')
The draws below stay inside these ranges and needn't reach their ends.
All inputs are finite; a program needn't handle non-finite values.
Results may differ from the reference program's by a relative error of at most 0.00023.
Values sent between devices are 32-bit elements; how exact they have to be, the bound alone decides.
No kernel may reach another device: no remote copies, remote signals or barrier semaphores. Data moves between devices by JAX's collectives and lax.ppermute only.
A program may use at most 64 MiB of HBM per device.

```python
import jax
import jax.numpy as jnp
from jax import lax

GRID = 72
LOC = 2
BLK = 2
NBLK = 2
ORBS = 64
N_BAND = 32


def draw_orbitals(key, part):
    key = jax.random.fold_in(key, 7)
    shape = (ORBS, GRID, GRID * GRID)
    return jnp.clip(jax.random.normal(key, shape, jnp.float32), -4.0, 4.0)


def setup_inputs(seed: int = 0) -> dict:
    seeds = jax.random.split(jax.random.key(seed), 3)
    return {
        "orbitals": draw_orbitals(jax.random.fold_in(seeds[2], 71), 0),
        "block_owner": jax.random.randint(seeds[1], (NBLK,), 0, N_BAND).astype(jnp.int32),
    }


def coulomb(edge_cells):
    points = jnp.arange(edge_cells, dtype=jnp.int32)
    folded = jnp.where(points > edge_cells // 2, points - edge_cells, points)
    upper = folded[:edge_cells // 2 + 1]
    squared = folded[:, None, None] ** 2 + folded[None, :, None] ** 2 + upper[None, None, :] ** 2
    scale = jnp.sqrt(jnp.float32(edge_cells ** 3 / ORBS))
    return jnp.where(squared > 0, scale / jnp.maximum(squared, 1).astype(jnp.float32), jnp.float32(0.0))

def reference(orbitals, block_owner):
    orbital_grid = orbitals.reshape(ORBS, GRID, GRID, GRID)
    chosen = (block_owner[:, None] * LOC + jnp.arange(BLK, dtype=jnp.int32)[None, :]).reshape(-1).astype(jnp.int32)
    blocks = jnp.take(orbital_grid, chosen, axis=0)
    kernel = coulomb(GRID)

    def advance(running, orbital):
        density = orbital[None] * blocks
        spectrum = jnp.fft.rfftn(density, axes=(1, 2, 3))
        potential = jnp.fft.irfftn(spectrum * kernel, s=(GRID, GRID, GRID), axes=(1, 2, 3)).astype(jnp.float32)
        own_field = -lax.optimization_barrier(jnp.sum(blocks * potential, axis=0))
        return (running - orbital[None] * potential, own_field)
    running, fields = lax.scan(advance, jnp.zeros_like(blocks), orbital_grid)
    return (fields.reshape(ORBS, GRID, GRID * GRID), running.reshape(NBLK, BLK, GRID, GRID * GRID))
```

```python
import math

import jax
import jax.numpy as jnp
import numpy as np
from jax import lax
from jax.experimental import pallas as pl
from jax.experimental.pallas import tpu as pltpu
from jax.sharding import PartitionSpec as P

GRID = 72
HALF = GRID // 2 + 1
KX = 40
PLANE = GRID * GRID
TILES = 41
LANES = 128
SLAB = 9
TAIL = 8 * TILES
ROWS = 384
XR = 80
BAND = 32
CHUNK = 2 * ROWS // BAND
SHARE = PLANE // BAND
PACK = 56
F32 = jnp.float32
BF16 = jnp.bfloat16
PARAMS = pltpu.CompilerParams(vmem_limit_bytes=48 * 1024 * 1024)


def split_np(table):
    high = table.astype(jnp.bfloat16)
    low = (table - high.astype(np.float64)).astype(jnp.bfloat16)
    return high, low


def tables():
    k = np.arange(GRID)
    ang = 2.0 * np.pi / GRID * ((k[:, None] * k[None, :]) % GRID)
    cos, sin = np.cos(ang), np.sin(ang)
    place = np.arange(GRID)
    plane = np.where(place < 64, SLAB * (place // 8) + place % 8, SLAB * (place - 64) + 8)
    forward_x = np.zeros((2 * KX, XR))
    forward_x[:HALF, :GRID] = cos[:HALF][:, plane]
    forward_x[KX : KX + HALF, :GRID] = -sin[:HALF][:, plane]
    weight = np.where((k[:HALF] == 0) | (k[:HALF] == GRID // 2), 1.0, 2.0) / GRID**3
    inverse_x = np.zeros((XR, 2 * KX))
    inverse_x[:GRID, :HALF] = (weight[:, None] * cos[:HALF][:, plane]).T
    inverse_x[:GRID, KX : KX + HALF] = -(weight[:, None] * sin[:HALF][:, plane]).T
    along_z = np.zeros((LANES, 2 * LANES))
    along_z[:GRID, :GRID] = cos
    along_z[:GRID, LANES : LANES + GRID] = sin
    forward_y = np.block([[cos, sin], [-sin, cos]])
    inverse_y = np.block([[cos, -sin], [sin, cos]])

    def left(table):
        high, low = split_np(table)
        return np.concatenate([high, high, low], axis=1)

    z_high, z_low = split_np(along_z)
    z_two = np.concatenate([z_high, z_high], axis=0)
    fold = np.where(k > GRID // 2, k - GRID, k).astype(np.float64)
    squares = np.ones((GRID, LANES))
    squares[:, :GRID] = fold[:, None] ** 2 + fold[None, :] ** 2
    return (
        left(forward_x),
        left(inverse_x),
        z_two,
        z_low,
        left(forward_y),
        left(inverse_y),
        squares.astype(np.float32),
    )


def split(x):
    high = x.astype(BF16)
    low = (x - high.astype(F32)).astype(BF16)
    return high, low


def left_dot(table, x):
    high, low = split(x)
    return jnp.dot(table, jnp.concatenate([high, low, high], axis=0), preferred_element_type=F32)


def right_dot(x, two, low_table):
    high, low = split(x)
    both = jnp.concatenate([high, low], axis=1)
    return jnp.dot(both, two, preferred_element_type=F32) + jnp.dot(
        high, low_table, preferred_element_type=F32
    )


def pack_kernel(orb_ref, out_ref):
    for o in range(2):
        out_ref[o, TAIL:ROWS, :] = jnp.zeros((ROWS - TAIL, LANES), F32)
        for t in range(TILES):
            wide = min(LANES, PLANE - t * LANES)
            if wide < LANES:
                out_ref[o, 8 * t : 8 * t + 8, :] = jnp.zeros((8, LANES), F32)
            cols = slice(t * LANES, t * LANES + wide)
            out_ref[o, 8 * t : 8 * t + 8, :wide] = orb_ref[o, 0:8, cols]
            out_ref[o, TAIL + t : TAIL + t + 1, :wide] = orb_ref[o, 8:9, cols]


def pack(orbitals):
    return pl.pallas_call(
        pack_kernel,
        out_shape=jax.ShapeDtypeStruct((2, ROWS, LANES), F32),
        compiler_params=PARAMS,
    )(orbitals)


def field_kernel(
    scale,
    den_ref,
    fx_ref,
    ix_ref,
    ztwo_ref,
    zlow_ref,
    fy_ref,
    iy_ref,
    sq_ref,
    out_ref,
    wide_ref,
    col_ref,
    re_ref,
    im_ref,
):
    lane = lax.broadcasted_iota(jnp.int32, (XR, LANES), 1)

    wide_ref[GRID:XR, :] = jnp.zeros((XR - GRID, TILES * LANES), F32)
    for t in range(TILES):
        cols = slice(t * LANES, (t + 1) * LANES)
        for s in range(8):
            wide_ref[8 * s : 8 * s + 8, cols] = den_ref[s, 8 * t : 8 * t + 8, :]
            wide_ref[64 + s : 65 + s, cols] = den_ref[s, TAIL + t : TAIL + t + 1, :]
    for t in range(0, TILES, 4):
        cols = slice(t * LANES, min(t + 4, TILES) * LANES)
        wide_ref[:, cols] = left_dot(fx_ref[...], wide_ref[:, cols])

    for y in range(GRID):
        t, off = divmod(y * GRID, LANES)
        value = wide_ref[:, t * LANES : (t + 1) * LANES]
        if off:
            value = pltpu.roll(value, LANES - off, 1)
            if off + GRID > LANES:
                after = pltpu.roll(wide_ref[:, (t + 1) * LANES : (t + 2) * LANES], LANES - off, 1)
                value = jnp.where(lane < LANES - off, value, after)
        col_ref[y * XR : (y + 1) * XR, :] = value

    def forward_z(j, carry):
        base = pl.multiple_of(j * 8 * XR, 8 * XR)
        both = right_dot(col_ref[pl.ds(base, 8 * XR), :], ztwo_ref[...], zlow_ref[...])
        base = pl.multiple_of(j * 8 * KX, 8 * KX)
        for y in range(8):
            real = both[y * XR : y * XR + KX]
            imag = both[y * XR + KX : (y + 1) * XR]
            rows = pl.ds(base + y * KX, KX)
            re_ref[rows, :] = real[:, :LANES] + imag[:, LANES:]
            im_ref[rows, :] = imag[:, :LANES] - real[:, LANES:]
        return carry

    lax.fori_loop(0, GRID // 8, forward_z, 0)

    def along_y(j, carry):
        parts = []
        for q in range(2):
            rows = pl.ds(2 * j + q, GRID, stride=KX)
            parts.append(jnp.concatenate([re_ref[rows, :], im_ref[rows, :]], axis=0))
        spec = left_dot(fy_ref[...], jnp.concatenate(parts, axis=1))
        factors = []
        for q in range(2):
            kx = (2 * j + q).astype(F32)
            square = sq_ref[...] + kx * kx
            factor = jnp.where(square > 0, scale / jnp.maximum(square, 1.0), 0.0)
            factors.append(jnp.concatenate([factor, factor], axis=0))
        spec = spec * jnp.concatenate(factors, axis=1)
        back = left_dot(iy_ref[...], spec)
        for q in range(2):
            rows = pl.ds(2 * j + q, GRID, stride=KX)
            cols = slice(q * LANES, (q + 1) * LANES)
            re_ref[rows, :] = back[:GRID, cols]
            im_ref[rows, :] = back[GRID:, cols]
        return carry

    lax.fori_loop(0, (HALF + 1) // 2, along_y, 0)

    def inverse_z(j, carry):
        base = pl.multiple_of(j * 8 * KX, 8 * KX)
        rows = pl.ds(base, 8 * KX)
        real = right_dot(re_ref[rows, :], ztwo_ref[...], zlow_ref[...])
        imag = right_dot(im_ref[rows, :], ztwo_ref[...], zlow_ref[...])
        new_re = real[:, :LANES] - imag[:, LANES:]
        new_im = real[:, LANES:] + imag[:, :LANES]
        base = pl.multiple_of(j * 8 * XR, 8 * XR)
        for y in range(8):
            col_ref[pl.ds(base + y * XR, KX), :] = new_re[y * KX : (y + 1) * KX]
            col_ref[pl.ds(base + y * XR + KX, KX), :] = new_im[y * KX : (y + 1) * KX]
        return carry

    lax.fori_loop(0, GRID // 8, inverse_z, 0)

    for t in range(TILES):
        value = jnp.zeros((XR, LANES), F32)
        for y in range(GRID):
            at = y * GRID - t * LANES
            if at >= LANES or at + GRID <= 0:
                continue
            piece = col_ref[y * XR : (y + 1) * XR, :]
            if at % LANES:
                piece = pltpu.roll(piece, at % LANES, 1)
            keep = (lane >= at) & (lane < at + GRID)
            value = jnp.where(keep, piece, value)
        wide_ref[:, t * LANES : (t + 1) * LANES] = value
    for t in range(0, TILES, 4):
        last = min(t + 4, TILES)
        cols = slice(t * LANES, last * LANES)
        pot = left_dot(ix_ref[...], wide_ref[:, cols])
        for u in range(t, last):
            part = pot[:, (u - t) * LANES : (u - t + 1) * LANES]
            for s in range(8):
                out_ref[s, 8 * u : 8 * u + 8, :] = part[8 * s : 8 * s + 8]
                out_ref[s, TAIL + u : TAIL + u + 1, :] = part[64 + s : 65 + s]
    for s in range(8):
        out_ref[s, TAIL + TILES : ROWS, :] = jnp.zeros((ROWS - TAIL - TILES, LANES), F32)


def potentials(densities, scale):
    def body(*refs):
        field_kernel(scale, *refs)

    return pl.pallas_call(
        body,
        out_shape=jax.ShapeDtypeStruct((8, ROWS, LANES), F32),
        scratch_shapes=[
            pltpu.VMEM((XR, TILES * LANES), F32),
            pltpu.VMEM((GRID * XR, LANES), F32),
            pltpu.VMEM((GRID * KX, LANES), F32),
            pltpu.VMEM((GRID * KX, LANES), F32),
        ],
        compiler_params=PARAMS,
    )(densities, *[jnp.asarray(t) for t in tables()])


def sums_kernel(pot_ref, orb_ref, blk_ref, field_ref, share_ref, wide_ref):
    wide_ref[32:40, :] = jnp.zeros((8, TILES * LANES), F32)
    for i in range(2):
        for t in range(TILES + 1):
            tail = t == TILES
            rows = slice(TAIL, ROWS) if tail else slice(8 * t, 8 * t + 8)
            total = blk_ref[0, rows, :] * pot_ref[4 * i, rows, :]
            for b in range(1, 4):
                total = total + blk_ref[b, rows, :] * pot_ref[4 * i + b, rows, :]
            total = -total
            if tail:
                for u in range(TILES):
                    wide = min(LANES, PLANE - u * LANES)
                    field_ref[i, 8:9, u * LANES : u * LANES + wide] = total[u : u + 1, :wide]
            else:
                wide = min(LANES, PLANE - t * LANES)
                field_ref[i, 0:8, t * LANES : t * LANES + wide] = total[:, :wide]
    for b in range(4):
        for t in range(TILES + 1):
            tail = t == TILES
            rows = slice(TAIL, ROWS) if tail else slice(8 * t, 8 * t + 8)
            total = -(
                orb_ref[0, rows, :] * pot_ref[b, rows, :]
                + orb_ref[1, rows, :] * pot_ref[4 + b, rows, :]
            )
            if tail:
                for u in range(TILES):
                    wide_ref[32 + b : 33 + b, u * LANES : (u + 1) * LANES] = total[u : u + 1]
            else:
                wide_ref[8 * b : 8 * b + 8, t * LANES : (t + 1) * LANES] = total
    lane = lax.broadcasted_iota(jnp.int32, (40, LANES), 1)
    rest = SHARE - LANES

    def cut(start):
        t, off = divmod(start, LANES)
        value = wide_ref[:, t * LANES : (t + 1) * LANES]
        if off:
            value = pltpu.roll(value, LANES - off, 1)
            if t + 1 < TILES:
                after = pltpu.roll(wide_ref[:, (t + 1) * LANES : (t + 2) * LANES], LANES - off, 1)
                value = jnp.where(lane < LANES - off, value, after)
        return value

    for r in range(BAND):
        share_ref[r, 0:40, :] = cut(r * SHARE)
        more = cut(r * SHARE + LANES)
        low, mid, top = more[0:16], more[16:32], more[32:40]
        mid = pltpu.roll(mid, rest, 1)
        top = jnp.concatenate([pltpu.roll(top, 2 * rest, 1), jnp.zeros((8, LANES), F32)], axis=0)
        where = lane[:16]
        share_ref[r, 40:56, :] = jnp.where(
            where < rest, low, jnp.where(where < 2 * rest, mid, top)
        )


def sums(pot, packed, blocks):
    return pl.pallas_call(
        sums_kernel,
        out_shape=(
            jax.ShapeDtypeStruct((2, SLAB, PLANE), F32),
            jax.ShapeDtypeStruct((BAND, PACK, LANES), F32),
        ),
        scratch_shapes=[pltpu.VMEM((40, TILES * LANES), F32)],
        compiler_params=PARAMS,
    )(pot, packed, blocks)


def share_kernel(part_ref, out_ref):
    total = part_ref[0]
    for r in range(1, BAND):
        total = total + part_ref[r]
    rest = SHARE - LANES
    tail = total[40:56]
    tails = [tail, pltpu.roll(tail, LANES - rest, 1), pltpu.roll(tail, LANES - 2 * rest, 1)]
    for b in range(4):
        at = (b // 2, b % 2)
        out_ref[at[0], at[1], 0:8, :LANES] = total[8 * b : 8 * b + 8]
        more = tails[b // 2][8 * (b % 2) : 8 * (b % 2) + 8]
        out_ref[at[0], at[1], 0:8, LANES:SHARE] = more[:, :rest]
        out_ref[at[0], at[1], 8:9, :LANES] = total[32 + b : 33 + b]
        out_ref[at[0], at[1], 8:9, LANES:SHARE] = tails[2][b : b + 1, :rest]


def share(parts):
    return pl.pallas_call(
        share_kernel,
        out_shape=jax.ShapeDtypeStruct((2, 2, SLAB, SHARE), F32),
        compiler_params=PARAMS,
    )(parts)


def on_device(orbitals, block_owner):
    scale = math.sqrt(GRID**3 / (2 * BAND))
    packed = pack(orbitals)
    pieces = lax.all_to_all(packed.reshape(BAND, CHUNK, LANES), "band", 0, 0)
    mine = jnp.take(pieces, block_owner, axis=0, mode="clip")
    spread = jnp.broadcast_to(mine[None], (BAND, 2, CHUNK, LANES))
    gathered = lax.all_to_all(spread, "band", 0, 0)
    blocks = gathered.transpose(1, 0, 2, 3).reshape(4, ROWS, LANES)
    densities = (packed[:, None] * blocks[None]).reshape(8, ROWS, LANES)
    whole = lax.all_to_all(densities, "grid", 0, 0)
    pot = potentials(whole, scale)
    pot = lax.all_to_all(pot, "grid", 0, 0)
    field, shares = sums(pot, packed, blocks)
    block_field = share(lax.all_to_all(shares, "band", 0, 0))
    return field, block_field


def solution(mesh):
    return jax.shard_map(
        on_device,
        mesh=mesh,
        in_specs=(P("band", "grid", None), P()),
        out_specs=(P("band", "grid", None), P(None, None, "grid", "band")),
        check_vma=False,
    )
```

```python
import math

import jax
import jax.numpy as jnp
import numpy as np
from jax import lax
from jax.experimental import pallas as pl
from jax.experimental.pallas import tpu as pltpu
from jax.sharding import PartitionSpec as P

GRID = 72
HALF = GRID // 2 + 1
KX = 40
PLANE = GRID * GRID
TILES = 41
LANES = 128
SLAB = 9
TAIL = 8 * TILES
ROWS = 384
XR = 80
BAND = 32
QUARTER = ROWS // 4
PIECE = ROWS // 8
SHARE = PLANE // BAND
REST = SHARE - LANES
PACK = 96
PART = 24
F32 = jnp.float32
BF16 = jnp.bfloat16
PARAMS = pltpu.CompilerParams(vmem_limit_bytes=48 * 1024 * 1024)


def split_np(table):
    high = table.astype(jnp.bfloat16)
    low = (table - high.astype(np.float64)).astype(jnp.bfloat16)
    return high, low


def tables():
    k = np.arange(GRID)
    ang = 2.0 * np.pi / GRID * ((k[:, None] * k[None, :]) % GRID)
    cos, sin = np.cos(ang), np.sin(ang)
    place = np.arange(GRID)
    plane = np.where(place < 64, SLAB * (place // 8) + place % 8, SLAB * (place - 64) + 8)
    forward_x = np.zeros((2 * KX, XR))
    forward_x[:HALF, :GRID] = cos[:HALF][:, plane]
    forward_x[KX : KX + HALF, :GRID] = -sin[:HALF][:, plane]
    weight = np.where((k[:HALF] == 0) | (k[:HALF] == GRID // 2), 1.0, 2.0) / GRID**3
    inverse_x = np.zeros((XR, 2 * KX))
    inverse_x[:GRID, :HALF] = (weight[:, None] * cos[:HALF][:, plane]).T
    inverse_x[:GRID, KX : KX + HALF] = -(weight[:, None] * sin[:HALF][:, plane]).T
    along_z = np.zeros((LANES, 2 * LANES))
    along_z[:GRID, :GRID] = cos
    along_z[:GRID, LANES : LANES + GRID] = sin
    forward_y = np.block([[cos, sin], [-sin, cos]])
    inverse_y = np.block([[cos, -sin], [sin, cos]])

    def left(table):
        high, low = split_np(table)
        return np.concatenate([high, high, low], axis=1)

    z_high, z_low = split_np(along_z)
    z_two = np.concatenate([z_high, z_high], axis=0)
    fold = np.where(k > GRID // 2, k - GRID, k).astype(np.float64)
    squares = np.ones((GRID, LANES))
    squares[:, :GRID] = fold[:, None] ** 2 + fold[None, :] ** 2
    return (
        left(forward_x),
        left(inverse_x),
        z_two,
        z_low,
        left(forward_y),
        left(inverse_y),
        squares.astype(np.float32),
    )


def split(x):
    high = x.astype(BF16)
    low = (x - high.astype(F32)).astype(BF16)
    return high, low


def left_dot(table, x):
    high, low = split(x)
    return jnp.dot(table, jnp.concatenate([high, low, high], axis=0), preferred_element_type=F32)


def right_dot(x, two, low_table):
    high, low = split(x)
    both = jnp.concatenate([high, low], axis=1)
    return jnp.dot(both, two, preferred_element_type=F32) + jnp.dot(
        high, low_table, preferred_element_type=F32
    )


def pick(index, choices):
    value = choices[0]
    for d in range(1, len(choices)):
        value = jnp.where(index == d, choices[d], value)
    return value


def shape(*dims):
    return jax.ShapeDtypeStruct(dims, F32)


def call(kernel, out_shape, info, *arrays, scratch=(), flops=0):
    specs = [pl.BlockSpec(memory_space=pltpu.SMEM)]
    specs += [pl.BlockSpec(memory_space=pltpu.VMEM) for _ in arrays]
    size = sum(a.size for a in arrays) * 4
    return pl.pallas_call(
        kernel,
        in_specs=specs,
        out_shape=out_shape,
        scratch_shapes=list(scratch),
        compiler_params=PARAMS,
        cost_estimate=pl.CostEstimate(flops=flops, bytes_accessed=2 * size, transcendentals=0),
    )(info, *arrays)


MY_X, MY_C, MY_Z, X_STEP, C_OWN, Z_STEP = 0, 1, 2, 3, 5, 7


def pack_kernel(info, orb_ref, out_ref, *quarters):
    for o in range(2):
        out_ref[o, TAIL:ROWS, :] = jnp.zeros((ROWS - TAIL, LANES), F32)
        for t in range(TILES):
            wide = min(LANES, PLANE - t * LANES)
            if wide < LANES:
                out_ref[o, 8 * t : 8 * t + 8, :] = jnp.zeros((8, LANES), F32)
            cols = slice(t * LANES, t * LANES + wide)
            out_ref[o, 8 * t : 8 * t + 8, :wide] = orb_ref[o, 0:8, cols]
            out_ref[o, TAIL + t : TAIL + t + 1, :wide] = orb_ref[o, 8:9, cols]
    for d in range(4):
        first = pl.multiple_of(QUARTER * lax.rem(info[MY_X] + d, 4), QUARTER)
        for o in range(2):
            quarters[d][o] = out_ref[o, pl.ds(first, QUARTER), :]


def pick_x_kernel(info, q0, q1, q2, q3, keep_ref, give_ref):
    for ref, half in ((keep_ref, info[MY_C]), (give_ref, 1 - info[MY_C])):
        rows = pl.ds(pl.multiple_of(half * PIECE, PIECE), PIECE)
        for step in range(2):
            for m in range(2):
                choices = [q[m, rows, :] for q in (q0, q1, q2, q3)]
                ref[2 * step + m] = pick(info[X_STEP + step], choices)


def pick_core_kernel(info, keep_ref, got_ref, out_ref):
    for b in range(4):
        out_ref[b] = jnp.where(info[C_OWN + b // 2] == 1, keep_ref[b], got_ref[b])


def pick_z_kernel(info, z0, z1, z2, z3, out_ref):
    for b in range(4):
        value = pick(info[Z_STEP + b // 2], [z[b] for z in (z0, z1, z2, z3)])
        out_ref[b] = value
        out_ref[4 + b] = value


def field_kernel(
    scale,
    info,
    orb_ref,
    p0,
    p1,
    p2,
    p3,
    c0,
    c1,
    c2,
    c3,
    fx_ref,
    ix_ref,
    ztwo_ref,
    zlow_ref,
    fy_ref,
    iy_ref,
    sq_ref,
    own_ref,
    k0,
    k1,
    k2,
    k3,
    g0,
    g1,
    g2,
    g3,
    blk_ref,
    wide_ref,
    orb_tail,
    blk_tail,
    col_ref,
    re_ref,
    im_ref,
):
    lane = lax.broadcasted_iota(jnp.int32, (XR, LANES), 1)

    for d, (mine, other) in enumerate(((p0, c0), (p1, c1), (p2, c2), (p3, c3))):
        quarter = QUARTER * lax.rem(info[MY_X] + 4 - d, 4)
        for ref, half in ((mine, info[MY_C]), (other, 1 - info[MY_C])):
            rows = pl.ds(pl.multiple_of(quarter + PIECE * half, PIECE), PIECE)
            for s in range(8):
                blk_ref[s, rows, :] = ref[s]

    wide_ref[GRID:XR, :] = jnp.zeros((XR - GRID, (TILES + 2) * LANES), F32)
    for t in range(TILES):
        cols = slice(t * LANES, (t + 1) * LANES)
        rows = slice(8 * t, 8 * t + 8)
        for s in range(8):
            wide_ref[8 * s : 8 * s + 8, cols] = orb_ref[s, rows, :] * blk_ref[s, rows, :]
            orb_tail[s : s + 1, cols] = orb_ref[s, TAIL + t : TAIL + t + 1, :]
            blk_tail[s : s + 1, cols] = blk_ref[s, TAIL + t : TAIL + t + 1, :]
        wide_ref[64:72, cols] = orb_tail[:, cols] * blk_tail[:, cols]
    for t in range(0, TILES, 4):
        cols = slice(t * LANES, min(t + 4, TILES) * LANES)
        wide_ref[:, cols] = left_dot(fx_ref[...], wide_ref[:, cols])

    for y in range(GRID):
        t, off = divmod(y * GRID, LANES)
        value = wide_ref[:, t * LANES : (t + 1) * LANES]
        if off:
            value = pltpu.roll(value, LANES - off, 1)
            if off + GRID > LANES:
                after = pltpu.roll(wide_ref[:, (t + 1) * LANES : (t + 2) * LANES], LANES - off, 1)
                value = jnp.where(lane < LANES - off, value, after)
        col_ref[y * XR : (y + 1) * XR, :] = value

    def forward_z(j, carry):
        base = pl.multiple_of(j * 8 * XR, 8 * XR)
        both = right_dot(col_ref[pl.ds(base, 8 * XR), :], ztwo_ref[...], zlow_ref[...])
        base = pl.multiple_of(j * 8 * KX, 8 * KX)
        for y in range(8):
            real = both[y * XR : y * XR + KX]
            imag = both[y * XR + KX : (y + 1) * XR]
            rows = pl.ds(base + y * KX, KX)
            re_ref[rows, :] = real[:, :LANES] + imag[:, LANES:]
            im_ref[rows, :] = imag[:, :LANES] - real[:, LANES:]
        return carry

    lax.fori_loop(0, GRID // 8, forward_z, 0)

    def along_y(j, carry):
        parts = []
        for q in range(2):
            rows = pl.ds(2 * j + q, GRID, stride=KX)
            parts.append(jnp.concatenate([re_ref[rows, :], im_ref[rows, :]], axis=0))
        spec = left_dot(fy_ref[...], jnp.concatenate(parts, axis=1))
        factors = []
        for q in range(2):
            kx = (2 * j + q).astype(F32)
            square = sq_ref[...] + kx * kx
            factor = jnp.where(square > 0, scale / jnp.maximum(square, 1.0), 0.0)
            factors.append(jnp.concatenate([factor, factor], axis=0))
        spec = spec * jnp.concatenate(factors, axis=1)
        back = left_dot(iy_ref[...], spec)
        for q in range(2):
            rows = pl.ds(2 * j + q, GRID, stride=KX)
            cols = slice(q * LANES, (q + 1) * LANES)
            re_ref[rows, :] = back[:GRID, cols]
            im_ref[rows, :] = back[GRID:, cols]
        return carry

    lax.fori_loop(0, (HALF + 1) // 2, along_y, 0)

    def inverse_z(j, carry):
        base = pl.multiple_of(j * 8 * KX, 8 * KX)
        rows = pl.ds(base, 8 * KX)
        real = right_dot(re_ref[rows, :], ztwo_ref[...], zlow_ref[...])
        imag = right_dot(im_ref[rows, :], ztwo_ref[...], zlow_ref[...])
        new_re = real[:, :LANES] - imag[:, LANES:]
        new_im = real[:, LANES:] + imag[:, :LANES]
        base = pl.multiple_of(j * 8 * XR, 8 * XR)
        for y in range(8):
            col_ref[pl.ds(base + y * XR, KX), :] = new_re[y * KX : (y + 1) * KX]
            col_ref[pl.ds(base + y * XR + KX, KX), :] = new_im[y * KX : (y + 1) * KX]
        return carry

    lax.fori_loop(0, GRID // 8, inverse_z, 0)

    for t in range(TILES):
        value = jnp.zeros((XR, LANES), F32)
        for y in range(GRID):
            at = y * GRID - t * LANES
            if at >= LANES or at + GRID <= 0:
                continue
            piece = col_ref[y * XR : (y + 1) * XR, :]
            if at % LANES:
                piece = pltpu.roll(piece, at % LANES, 1)
            keep = (lane >= at) & (lane < at + GRID)
            value = jnp.where(keep, piece, value)
        wide_ref[:, t * LANES : (t + 1) * LANES] = value

    for s in range(8):
        own_ref[s, TAIL + TILES : ROWS, :] = jnp.zeros((ROWS - TAIL - TILES, LANES), F32)
    for t in range(0, TILES, 4):
        last = min(t + 4, TILES)
        cols = slice(t * LANES, last * LANES)
        pot = -left_dot(ix_ref[...], wide_ref[:, cols])
        for u in range(t, last):
            part = pot[:, (u - t) * LANES : (u - t + 1) * LANES]
            rows = slice(8 * u, 8 * u + 8)
            one = slice(u * LANES, (u + 1) * LANES)
            tail = part[64:72] * blk_tail[:, one]
            for s in range(8):
                piece = part[8 * s : 8 * s + 8]
                own_ref[s, rows, :] = piece * blk_ref[s, rows, :]
                own_ref[s, TAIL + u : TAIL + u + 1, :] = tail[s : s + 1]
                wide_ref[8 * s : 8 * s + 8, one] = piece * orb_ref[s, rows, :]
            wide_ref[64:72, one] = part[64:72] * orb_tail[:, one]
    wide_ref[:, TILES * LANES :] = jnp.zeros((XR, 2 * LANES), F32)

    def cut(start):
        t = start // LANES
        off = start - t * LANES
        turn = lax.rem(LANES - off, LANES)
        cols = [pl.ds(pl.multiple_of((t + k) * LANES, LANES), LANES) for k in range(3)]
        rolled = [pltpu.roll(wide_ref[:GRID, c], turn, 1) for c in cols]
        keep = lane[:GRID] < LANES - off
        return jnp.where(keep, rolled[0], rolled[1]), jnp.where(keep, rolled[1], rolled[2])

    third = lane[:8]
    for x in range(4):
        for core, ref in ((0, (k0, k1, k2, k3)[x]), (1, (g0, g1, g2, g3)[x])):

            def share_out(z, carry, x=x, core=core, ref=ref):
                band = 8 * lax.rem(info[MY_Z] + z, 4) + 2 * lax.rem(info[MY_X] + x, 4)
                band = band + lax.rem(info[MY_C] + core, 2)
                head, rest = cut(band * SHARE)
                ref[z, :GRID, :] = head
                for j in range(3):
                    a, b, c = (rest[8 * (3 * j + k) : 8 * (3 * j + k) + 8] for k in range(3))
                    b, c = pltpu.roll(b, REST, 1), pltpu.roll(c, 2 * REST, 1)
                    packed = jnp.where(third < REST, a, jnp.where(third < 2 * REST, b, c))
                    ref[z, GRID + 8 * j : GRID + 8 * j + 8, :] = packed
                return carry

            lax.fori_loop(0, 4, share_out, 0)


def fields(info, orbital, pieces, scale):
    def body(*refs):
        field_kernel(scale, *refs)

    return call(
        body,
        [shape(8, ROWS, LANES)] + [shape(4, PACK, LANES)] * 8,
        info,
        orbital,
        *pieces,
        *[jnp.asarray(t) for t in tables()],
        scratch=[
            pltpu.VMEM((8, ROWS, LANES), F32),
            pltpu.VMEM((XR, (TILES + 2) * LANES), F32),
            pltpu.VMEM((8, TILES * LANES), F32),
            pltpu.VMEM((8, TILES * LANES), F32),
            pltpu.VMEM((GRID * XR, LANES), F32),
            pltpu.VMEM((GRID * KX, LANES), F32),
            pltpu.VMEM((GRID * KX, LANES), F32),
        ],
        flops=10**10,
    )


def add_kernel(info, a_ref, b_ref, out_ref):
    out_ref[...] = a_ref[...] + b_ref[...]


def add_x_kernel(info, k_ref, g_ref, r1, r2, r3, *outs):
    for z in range(4):
        outs[z][...] = k_ref[z] + g_ref[z] + r1[z] + r2[z] + r3[z]


def add_z_kernel(info, s_ref, r1, r2, r3, out_ref, sum_ref):
    sum_ref[...] = s_ref[...] + r1[...] + r2[...] + r3[...]
    out_ref[...] = jnp.zeros((8, PART, LANES), F32)

    def rest(tile):
        value = sum_ref[GRID + 8 * (tile // 3) : GRID + 8 * (tile // 3) + 8, :]
        turn = tile % 3 * REST
        return pltpu.roll(value, LANES - turn, 1) if turn else value

    last = rest(8)
    for s in range(8):
        out_ref[s, 0:8, :] = sum_ref[8 * s : 8 * s + 8, :]
        out_ref[s, 8:16, :] = rest(s)
        out_ref[s, 16:17, :] = sum_ref[64 + s : 65 + s, :]
        out_ref[s, 17:18, :] = last[s : s + 1]


def share_kernel(info, part_ref, out_ref):
    for b in range(4):
        total = part_ref[b] + part_ref[4 + b]
        at = (b // 2, b % 2)
        out_ref[at[0], at[1], 0:8, :LANES] = total[0:8]
        out_ref[at[0], at[1], 0:8, LANES:SHARE] = total[8:16, :REST]
        out_ref[at[0], at[1], 8:9, :LANES] = total[16:17]
        out_ref[at[0], at[1], 8:9, LANES:SHARE] = total[17:18, :REST]


def own_kernel(info, part_ref, out_ref):
    for i in range(2):
        for t in range(TILES + 1):
            rows = slice(TAIL, ROWS) if t == TILES else slice(8 * t, 8 * t + 8)
            total = part_ref[4 * i, rows, :]
            for b in range(1, 4):
                total = total + part_ref[4 * i + b, rows, :]
            if t == TILES:
                for u in range(TILES):
                    wide = min(LANES, PLANE - u * LANES)
                    out_ref[i, 8:9, u * LANES : u * LANES + wide] = total[u : u + 1, :wide]
            else:
                wide = min(LANES, PLANE - t * LANES)
                out_ref[i, 0:8, t * LANES : t * LANES + wide] = total[:, :wide]


def shift_x(d):
    return [(i, i // 8 * 8 + (i // 2 + d) % 4 * 2 + i % 2) for i in range(BAND)]


def shift_z(d):
    return [(i, (i + 8 * d) % BAND) for i in range(BAND)]


def other_core(x):
    return lax.ppermute(x, "band", [(i, i ^ 1) for i in range(BAND)])


def scalars(block_owner):
    me = lax.axis_index("band")
    owner = jnp.clip(block_owner, 0, BAND - 1)
    x, c, z = me // 2 % 4, me % 2, me // 8
    parts = [
        jnp.stack([x, c, z]),
        (x - owner // 2 % 4) % 4,
        (c == owner % 2).astype(jnp.int32),
        (z - owner // 8) % 4,
    ]
    return jnp.concatenate([p.astype(jnp.int32) for p in parts])


def on_device(orbitals, block_owner):
    scale = math.sqrt(GRID**3 / (2 * BAND))
    info = scalars(block_owner)
    packed, *quarters = call(
        pack_kernel, [shape(2, ROWS, LANES)] + [shape(2, QUARTER, LANES)] * 4, info, orbitals
    )
    spread = jnp.broadcast_to(packed[:, None], (2, 4, ROWS, LANES)).reshape(8, ROWS, LANES)
    orbital = lax.all_to_all(spread, "grid", 0, 0)

    quarters = quarters[:1] + [lax.ppermute(quarters[d], "band", shift_x(d)) for d in (1, 2, 3)]
    half = shape(4, PIECE, LANES)
    keep, give = call(pick_x_kernel, [half, half], info, *quarters)
    mine = call(pick_core_kernel, half, info, keep, other_core(give))
    along = [mine] + [lax.ppermute(mine, "band", shift_z(d)) for d in (1, 2, 3)]
    mine = call(pick_z_kernel, shape(8, PIECE, LANES), info, *along)
    piece = lax.all_to_all(mine, "grid", 0, 0)
    pieces = [piece] + [lax.ppermute(piece, "band", shift_x(d)) for d in (1, 2, 3)]
    pieces = pieces + [other_core(p) for p in pieces]

    own, *shares = fields(info, orbital, pieces, scale)
    field = call(
        own_kernel, shape(2, SLAB, PLANE), info, lax.all_to_all(own, "grid", 0, 0)
    )
    kept, got = shares[:4], [other_core(g) for g in shares[4:]]
    part = shape(4, PACK, LANES)
    moved = []
    for d in (1, 2, 3):
        moved.append(lax.ppermute(call(add_kernel, part, info, kept[d], got[d]), "band", shift_x(d)))
    sums = call(add_x_kernel, [shape(PACK, LANES)] * 4, info, kept[0], got[0], *moved)
    moved = [lax.ppermute(sums[d], "band", shift_z(d)) for d in (1, 2, 3)]
    slabs = call(
        add_z_kernel,
        shape(8, PART, LANES),
        info,
        sums[0],
        *moved,
        scratch=[pltpu.VMEM((PACK, LANES), F32)],
    )
    block_field = call(
        share_kernel, shape(2, 2, SLAB, SHARE), info, lax.all_to_all(slabs, "grid", 0, 0)
    )
    return field, block_field


def solution(mesh):
    return jax.shard_map(
        on_device,
        mesh=mesh,
        in_specs=(P("band", "grid", None), P()),
        out_specs=(P("band", "grid", None), P(None, None, "grid", "band")),
        check_vma=False,
    )
```

```python
import math
import types

import jax
import jax.numpy as jnp
import numpy as np
from jax import lax
from jax.experimental import pallas as pl
from jax.experimental.pallas import tpu as pltpu
from jax.sharding import PartitionSpec as P

GRID = 72
HALF = GRID // 2 + 1
LINES = 72
GROUP = 20
KX = 40
PLANE = GRID * GRID
TILES = 41
LANES = 128
SLAB = 9
TAIL = 8 * TILES
ROWS = 384
XR = 80
BAND = 32
QUARTER = ROWS // 4
PIECE = ROWS // 8
SHARE = PLANE // BAND
REST = SHARE - LANES
PACK = 96
PART = 24
F32 = jnp.float32
BF16 = jnp.bfloat16
PARAMS = pltpu.CompilerParams(vmem_limit_bytes=48 * 1024 * 1024)


def split_np(table):
    high = table.astype(jnp.bfloat16)
    low = (table - high.astype(np.float64)).astype(jnp.bfloat16)
    return high, low


def tables():
    k = np.arange(GRID)
    ang = 2.0 * np.pi / GRID * ((k[:, None] * k[None, :]) % GRID)
    cos, sin = np.cos(ang), np.sin(ang)
    place = np.arange(GRID)
    plane = np.where(place < 64, SLAB * (place // 8) + place % 8, SLAB * (place - 64) + 8)
    forward_x = np.zeros((2 * KX, XR))
    forward_x[:HALF, :GRID] = cos[:HALF][:, plane]
    forward_x[KX : KX + HALF, :GRID] = -sin[:HALF][:, plane]
    weight = np.where((k[:HALF] == 0) | (k[:HALF] == GRID // 2), 1.0, 2.0) / GRID**3
    inverse_x = np.zeros((XR, 2 * KX))
    inverse_x[:GRID, :HALF] = (weight[:, None] * cos[:HALF][:, plane]).T
    inverse_x[:GRID, KX : KX + HALF] = -(weight[:, None] * sin[:HALF][:, plane]).T
    along_z = np.zeros((LANES, 2 * LANES))
    along_z[:GRID, :GRID] = cos
    along_z[:GRID, LANES : LANES + GRID] = sin
    forward_y = np.block([[cos, sin], [-sin, cos]])
    inverse_y = np.block([[cos, -sin], [sin, cos]])

    def left(table):
        high, low = split_np(table)
        return np.concatenate([high, high, low], axis=1)

    z_high, z_low = split_np(along_z)
    z_three = np.concatenate([z_high, z_high, z_low], axis=0)
    fold = np.where(k > GRID // 2, k - GRID, k).astype(np.float64)
    squares = np.ones((GRID, LANES))
    squares[:, :GRID] = fold[:, None] ** 2 + fold[None, :] ** 2
    return (
        left(forward_x),
        left(inverse_x),
        z_three,
        left(forward_y),
        left(inverse_y),
        squares.astype(np.float32),
    )


def split(x):
    high = x.astype(BF16)
    low = (x - high.astype(F32)).astype(BF16)
    return high, low


def left_dot(table, x):
    high, low = split(x)
    return jnp.dot(table, jnp.concatenate([high, low, high], axis=0), preferred_element_type=F32)


def right_dot(x, table):
    high, low = split(x)
    three = jnp.concatenate([high, low, high], axis=1)
    return jnp.dot(three, table, preferred_element_type=F32)


def pick(index, choices):
    value = choices[0]
    for d in range(1, len(choices)):
        value = jnp.where(index == d, choices[d], value)
    return value


def shape(*dims):
    return jax.ShapeDtypeStruct(dims, F32)


def call(kernel, out_shape, info, *arrays, after=(), scratch=(), flops=0):
    specs = [pl.BlockSpec(memory_space=pltpu.SMEM)]
    specs += [pl.BlockSpec(memory_space=pltpu.VMEM) for _ in arrays]
    specs += [pl.BlockSpec(memory_space=pl.ANY) for _ in after]
    size = sum(a.size for a in arrays) * 4
    return pl.pallas_call(
        kernel,
        in_specs=specs,
        out_shape=out_shape,
        scratch_shapes=list(scratch),
        compiler_params=PARAMS,
        cost_estimate=pl.CostEstimate(flops=flops, bytes_accessed=2 * size, transcendentals=0),
    )(info, *arrays, *after)


MY_X, MY_C, MY_Z, X_STEP, C_OWN, Z_STEP = 0, 1, 2, 3, 5, 7


def pack_kernel(info, orb_ref, out_ref, *quarters):
    for o in range(2):
        out_ref[o, TAIL:ROWS, :] = jnp.zeros((ROWS - TAIL, LANES), F32)
        for t in range(TILES):
            wide = min(LANES, PLANE - t * LANES)
            if wide < LANES:
                out_ref[o, 8 * t : 8 * t + 8, :] = jnp.zeros((8, LANES), F32)
            cols = slice(t * LANES, t * LANES + wide)
            out_ref[o, 8 * t : 8 * t + 8, :wide] = orb_ref[o, 0:8, cols]
            out_ref[o, TAIL + t : TAIL + t + 1, :wide] = orb_ref[o, 8:9, cols]
    for d in range(4):
        first = pl.multiple_of(QUARTER * lax.rem(info[MY_X] + d, 4), QUARTER)
        for o in range(2):
            quarters[d][o] = out_ref[o, pl.ds(first, QUARTER), :]


def spread_kernel(info, packed_ref, after_ref, out_ref):
    for g in range(8):
        out_ref[g] = packed_ref[g // 4]


def pick_x_kernel(info, q0, q1, q2, q3, keep_ref, give_ref):
    for ref, half in ((keep_ref, info[MY_C]), (give_ref, 1 - info[MY_C])):
        rows = pl.ds(pl.multiple_of(half * PIECE, PIECE), PIECE)
        for step in range(2):
            for m in range(2):
                choices = [q[m, rows, :] for q in (q0, q1, q2, q3)]
                ref[2 * step + m] = pick(info[X_STEP + step], choices)


def pick_core_kernel(info, keep_ref, got_ref, out_ref):
    for b in range(4):
        out_ref[b] = jnp.where(info[C_OWN + b // 2] == 1, keep_ref[b], got_ref[b])


def pick_z_kernel(info, z0, z1, z2, z3, after_ref, out_ref):
    for b in range(4):
        value = pick(info[Z_STEP + b // 2], [z[b] for z in (z0, z1, z2, z3)])
        out_ref[b] = value
        out_ref[4 + b] = value


def whole_block(r, info, scale):
    for d in range(4):
        quarter = QUARTER * lax.rem(info[MY_X] + 4 - d, 4)
        for ref, half in ((r.mine[d], info[MY_C]), (r.other[d], 1 - info[MY_C])):
            rows = pl.ds(pl.multiple_of(quarter + PIECE * half, PIECE), PIECE)
            for s in range(8):
                r.blk[s, rows, :] = ref[s]


def density(r, info, scale):
    r.wide[GRID:XR, :] = jnp.zeros((XR - GRID, (TILES + 2) * LANES), F32)
    for t in range(TILES):
        cols = slice(t * LANES, (t + 1) * LANES)
        rows = slice(8 * t, 8 * t + 8)
        for s in range(8):
            r.wide[8 * s : 8 * s + 8, cols] = r.orb[s, rows, :] * r.blk[s, rows, :]
            r.orb_tail[s : s + 1, cols] = r.orb[s, TAIL + t : TAIL + t + 1, :]
            r.blk_tail[s : s + 1, cols] = r.blk[s, TAIL + t : TAIL + t + 1, :]
        r.wide[64:72, cols] = r.orb_tail[:, cols] * r.blk_tail[:, cols]


def forward_x(r, info, scale):
    for t in range(0, TILES, 4):
        cols = slice(t * LANES, min(t + 4, TILES) * LANES)
        r.wide[:, cols] = left_dot(r.fx[...], r.wide[:, cols])


def to_columns(r, info, scale):
    lane = lax.broadcasted_iota(jnp.int32, (XR, LANES), 1)
    for y in range(GRID):
        t, off = divmod(y * GRID, LANES)
        value = r.wide[:, t * LANES : (t + 1) * LANES]
        if off:
            value = pltpu.roll(value, LANES - off, 1)
            if off + GRID > LANES:
                after = pltpu.roll(r.wide[:, (t + 1) * LANES : (t + 2) * LANES], LANES - off, 1)
                value = jnp.where(lane < LANES - off, value, after)
        r.col[y * XR : (y + 1) * XR, :] = value


def forward_z(r, info, scale):
    def step(j, carry):
        base = pl.multiple_of(j * LINES * XR, LINES * XR)
        both = right_dot(r.col[pl.ds(base, LINES * XR), :], r.zt[...])
        base = pl.multiple_of(j * LINES * KX, LINES * KX)
        for y in range(LINES):
            real = both[y * XR : y * XR + KX]
            imag = both[y * XR + KX : (y + 1) * XR]
            rows = pl.ds(base + y * KX, KX)
            r.re[rows, :] = real[:, :LANES] + imag[:, LANES:]
            r.im[rows, :] = imag[:, :LANES] - real[:, LANES:]
        return carry

    lax.fori_loop(0, GRID // LINES, step, 0)


def along_y(r, info, scale):
    def step(j, carry):
        strides = [pl.ds(GROUP * j + q, GRID, stride=KX) for q in range(GROUP)]
        lines = [jnp.concatenate([r.re[s, :], r.im[s, :]], axis=0) for s in strides]
        spec = left_dot(r.fy[...], jnp.concatenate(lines, axis=1))
        factors = []
        for q in range(GROUP):
            kx = (GROUP * j + q).astype(F32)
            square = r.sq[...] + kx * kx
            factor = jnp.where(square > 0, scale / jnp.maximum(square, 1.0), 0.0)
            factors.append(jnp.concatenate([factor, factor], axis=0))
        spec = spec * jnp.concatenate(factors, axis=1)
        back = left_dot(r.iy[...], spec)
        for q, s in enumerate(strides):
            cols = slice(q * LANES, (q + 1) * LANES)
            r.re[s, :] = back[:GRID, cols]
            r.im[s, :] = back[GRID:, cols]
        return carry

    lax.fori_loop(0, KX // GROUP, step, 0)


def inverse_z(r, info, scale):
    def step(j, carry):
        base = pl.multiple_of(j * LINES * KX, LINES * KX)
        rows = pl.ds(base, LINES * KX)
        real = right_dot(r.re[rows, :], r.zt[...])
        imag = right_dot(r.im[rows, :], r.zt[...])
        new_re = real[:, :LANES] - imag[:, LANES:]
        new_im = real[:, LANES:] + imag[:, :LANES]
        base = pl.multiple_of(j * LINES * XR, LINES * XR)
        for y in range(LINES):
            r.col[pl.ds(base + y * XR, KX), :] = new_re[y * KX : (y + 1) * KX]
            r.col[pl.ds(base + y * XR + KX, KX), :] = new_im[y * KX : (y + 1) * KX]
        return carry

    lax.fori_loop(0, GRID // LINES, step, 0)


def from_columns(r, info, scale):
    lane = lax.broadcasted_iota(jnp.int32, (XR, LANES), 1)
    for t in range(TILES):
        value = jnp.zeros((XR, LANES), F32)
        for y in range(GRID):
            at = y * GRID - t * LANES
            if at >= LANES or at + GRID <= 0:
                continue
            piece = r.col[y * XR : (y + 1) * XR, :]
            if at % LANES:
                piece = pltpu.roll(piece, at % LANES, 1)
            keep = (lane >= at) & (lane < at + GRID)
            value = jnp.where(keep, piece, value)
        r.wide[:, t * LANES : (t + 1) * LANES] = value


def inverse_x(r, info, scale):
    for s in range(8):
        r.own[s, TAIL + TILES : ROWS, :] = jnp.zeros((ROWS - TAIL - TILES, LANES), F32)
    for t in range(0, TILES, 4):
        last = min(t + 4, TILES)
        cols = slice(t * LANES, last * LANES)
        pot = -left_dot(r.ix[...], r.wide[:, cols])
        for u in range(t, last):
            part = pot[:, (u - t) * LANES : (u - t + 1) * LANES]
            rows = slice(8 * u, 8 * u + 8)
            one = slice(u * LANES, (u + 1) * LANES)
            tail = part[64:72] * r.blk_tail[:, one]
            for s in range(8):
                piece = part[8 * s : 8 * s + 8]
                r.own[s, rows, :] = piece * r.blk[s, rows, :]
                r.own[s, TAIL + u : TAIL + u + 1, :] = tail[s : s + 1]
                r.wide[8 * s : 8 * s + 8, one] = piece * r.orb[s, rows, :]
            r.wide[64:72, one] = part[64:72] * r.orb_tail[:, one]
    r.wide[:, TILES * LANES :] = jnp.zeros((XR, 2 * LANES), F32)


def share_out(r, info, scale):
    lane = lax.broadcasted_iota(jnp.int32, (GRID, LANES), 1)
    third = lane[:8]

    def turned(tile, turn):
        value = r.wide[:GRID, tile * LANES : (tile + 1) * LANES]
        return pltpu.roll(value, turn, 1) if turn else value

    for band in range(BAND):
        z, x, c = band // 8, band // 2 % 4, band % 2
        core = lax.rem(c + info[MY_C], 2)
        place = 4 * core + lax.rem(x + 4 - info[MY_X], 4)
        z = lax.rem(z + 4 - info[MY_Z], 4)
        t, off = divmod(band * SHARE, LANES)
        turn = (LANES - off) % LANES
        first, second = turned(t, turn), turned(t + 1, turn)
        head, rest = jnp.where(lane < LANES - off, first, second), second
        if off + REST > LANES:
            rest = jnp.where(lane < LANES - off, second, turned(t + 2, turn))
        r.cut[place, z, :GRID, :] = head
        for j in range(3):
            one, two, three = (rest[8 * (3 * j + k) : 8 * (3 * j + k) + 8] for k in range(3))
            two, three = pltpu.roll(two, REST, 1), pltpu.roll(three, 2 * REST, 1)
            packed = jnp.where(third < REST, one, jnp.where(third < 2 * REST, two, three))
            r.cut[place, z, GRID + 8 * j : GRID + 8 * j + 8, :] = packed
    for x in range(4):
        r.keep[x][...] = r.cut[x]
        r.give[x][...] = r.cut[4 + x]


STAGES = (
    whole_block,
    density,
    forward_x,
    to_columns,
    forward_z,
    along_y,
    inverse_z,
    from_columns,
    inverse_x,
    share_out,
)


def field_kernel(scale, info, *refs):
    tables = ("fx", "ix", "zt", "fy", "iy", "sq")
    scratch = ("blk", "wide", "orb_tail", "blk_tail", "col", "re", "im", "cut")
    r = types.SimpleNamespace(orb=refs[0], mine=refs[1:5], other=refs[5:9], own=refs[15])
    r.keep, r.give = refs[16:20], refs[20:24]
    vars(r).update(zip(tables, refs[9:15]))
    vars(r).update(zip(scratch, refs[24:]))
    for stage in STAGES:
        stage(r, info, scale)


def fields(info, orbital, pieces, scale):
    def body(*refs):
        field_kernel(scale, *refs)

    return call(
        body,
        [shape(8, ROWS, LANES)] + [shape(4, PACK, LANES)] * 8,
        info,
        orbital,
        *pieces,
        *[jnp.asarray(t) for t in tables()],
        scratch=[
            pltpu.VMEM((8, ROWS, LANES), F32),
            pltpu.VMEM((XR, (TILES + 2) * LANES), F32),
            pltpu.VMEM((8, TILES * LANES), F32),
            pltpu.VMEM((8, TILES * LANES), F32),
            pltpu.VMEM((GRID * XR, LANES), F32),
            pltpu.VMEM((GRID * KX, LANES), F32),
            pltpu.VMEM((GRID * KX, LANES), F32),
            pltpu.VMEM((8, 4, PACK, LANES), F32),
        ],
        flops=10**10,
    )


def add_kernel(info, a_ref, b_ref, out_ref):
    out_ref[...] = a_ref[...] + b_ref[...]


def add_x_kernel(info, k_ref, g_ref, r1, r2, r3, *outs):
    for z in range(4):
        outs[z][...] = k_ref[z] + g_ref[z] + r1[z] + r2[z] + r3[z]


def add_z_kernel(info, s_ref, r1, r2, r3, after_ref, out_ref, sum_ref):
    sum_ref[...] = s_ref[...] + r1[...] + r2[...] + r3[...]
    out_ref[...] = jnp.zeros((8, PART, LANES), F32)

    def rest(tile):
        value = sum_ref[GRID + 8 * (tile // 3) : GRID + 8 * (tile // 3) + 8, :]
        turn = tile % 3 * REST
        return pltpu.roll(value, LANES - turn, 1) if turn else value

    last = rest(8)
    for s in range(8):
        out_ref[s, 0:8, :] = sum_ref[8 * s : 8 * s + 8, :]
        out_ref[s, 8:16, :] = rest(s)
        out_ref[s, 16:17, :] = sum_ref[64 + s : 65 + s, :]
        out_ref[s, 17:18, :] = last[s : s + 1]


def share_kernel(info, part_ref, out_ref):
    for b in range(4):
        total = part_ref[b] + part_ref[4 + b]
        at = (b // 2, b % 2)
        out_ref[at[0], at[1], 0:8, :LANES] = total[0:8]
        out_ref[at[0], at[1], 0:8, LANES:SHARE] = total[8:16, :REST]
        out_ref[at[0], at[1], 8:9, :LANES] = total[16:17]
        out_ref[at[0], at[1], 8:9, LANES:SHARE] = total[17:18, :REST]


def own_kernel(info, part_ref, out_ref):
    for i in range(2):
        for t in range(TILES + 1):
            rows = slice(TAIL, ROWS) if t == TILES else slice(8 * t, 8 * t + 8)
            total = part_ref[4 * i, rows, :]
            for b in range(1, 4):
                total = total + part_ref[4 * i + b, rows, :]
            if t == TILES:
                for u in range(TILES):
                    wide = min(LANES, PLANE - u * LANES)
                    out_ref[i, 8:9, u * LANES : u * LANES + wide] = total[u : u + 1, :wide]
            else:
                wide = min(LANES, PLANE - t * LANES)
                out_ref[i, 0:8, t * LANES : t * LANES + wide] = total[:, :wide]


def shift_x(d):
    return [(i, i // 8 * 8 + (i // 2 + d) % 4 * 2 + i % 2) for i in range(BAND)]


def shift_z(d):
    return [(i, (i + 8 * d) % BAND) for i in range(BAND)]


def other_core(x):
    return lax.ppermute(x, "band", [(i, i ^ 1) for i in range(BAND)])


def scalars(block_owner):
    me = lax.axis_index("band")
    owner = jnp.clip(block_owner, 0, BAND - 1)
    x, c, z = me // 2 % 4, me % 2, me // 8
    parts = [
        jnp.stack([x, c, z]),
        (x - owner // 2 % 4) % 4,
        (c == owner % 2).astype(jnp.int32),
        (z - owner // 8) % 4,
    ]
    return jnp.concatenate([p.astype(jnp.int32) for p in parts])


def on_device(orbitals, block_owner):
    scale = math.sqrt(GRID**3 / (2 * BAND))
    info = scalars(block_owner)
    packed, *quarters = call(
        pack_kernel, [shape(2, ROWS, LANES)] + [shape(2, QUARTER, LANES)] * 4, info, orbitals
    )
    quarters = quarters[:1] + [lax.ppermute(quarters[d], "band", shift_x(d)) for d in (1, 2, 3)]
    spread = call(spread_kernel, shape(8, ROWS, LANES), info, packed, after=quarters[1:2])
    orbital = lax.all_to_all(spread, "grid", 0, 0)
    half = shape(4, PIECE, LANES)
    keep, give = call(pick_x_kernel, [half, half], info, *quarters)
    mine = call(pick_core_kernel, half, info, keep, other_core(give))
    along = [mine] + [lax.ppermute(mine, "band", shift_z(d)) for d in (1, 2, 3)]
    mine = call(pick_z_kernel, shape(8, PIECE, LANES), info, *along, after=[orbital])
    piece = lax.all_to_all(mine, "grid", 0, 0)
    pieces = [piece] + [lax.ppermute(piece, "band", shift_x(d)) for d in (1, 2, 3)]
    pieces = pieces + [other_core(p) for p in pieces]

    own, *shares = fields(info, orbital, pieces, scale)
    own = lax.all_to_all(own, "grid", 0, 0)
    kept, got = shares[:4], [other_core(g) for g in shares[4:]]
    part = shape(4, PACK, LANES)
    moved = []
    for d in (1, 2, 3):
        moved.append(lax.ppermute(call(add_kernel, part, info, kept[d], got[d]), "band", shift_x(d)))
    sums = call(add_x_kernel, [shape(PACK, LANES)] * 4, info, kept[0], got[0], *moved)
    moved = [lax.ppermute(sums[d], "band", shift_z(d)) for d in (1, 2, 3)]
    slabs = call(
        add_z_kernel,
        shape(8, PART, LANES),
        info,
        sums[0],
        *moved,
        after=[own],
        scratch=[pltpu.VMEM((PACK, LANES), F32)],
    )
    block_field = call(
        share_kernel, shape(2, 2, SLAB, SHARE), info, lax.all_to_all(slabs, "grid", 0, 0)
    )
    field = call(own_kernel, shape(2, SLAB, PLANE), info, own)
    return field, block_field


def solution(mesh):
    return jax.shard_map(
        on_device,
        mesh=mesh,
        in_specs=(P("band", "grid", None), P()),
        out_specs=(P("band", "grid", None), P(None, None, "grid", "band")),
        check_vma=False,
    )
```

```python
import math
import types

import jax
import jax.numpy as jnp
import numpy as np
from jax import lax
from jax.experimental import pallas as pl
from jax.experimental.pallas import tpu as pltpu
from jax.sharding import PartitionSpec as P

GRID = 72
HALF = GRID // 2 + 1
LINES = 72
GROUP = 20
KX = 40
PLANE = GRID * GRID
TILES = 41
LANES = 128
SLAB = 9
TAIL = 8 * TILES
ROWS = 384
XR = 80
BAND = 32
QUARTER = ROWS // 4
PIECE = ROWS // 8
SHARE = PLANE // BAND
REST = SHARE - LANES
PACK = 96
PART = 24
F32 = jnp.float32
BF16 = jnp.bfloat16


def split_np(table):
    high = table.astype(jnp.bfloat16)
    low = (table - high.astype(np.float64)).astype(jnp.bfloat16)
    return high, low


def tables():
    k = np.arange(GRID)
    ang = 2.0 * np.pi / GRID * ((k[:, None] * k[None, :]) % GRID)
    cos, sin = np.cos(ang), np.sin(ang)
    place = np.arange(GRID)
    plane = np.where(place < 64, SLAB * (place // 8) + place % 8, SLAB * (place - 64) + 8)
    forward_x = np.zeros((2 * KX, XR))
    forward_x[:HALF, :GRID] = cos[:HALF][:, plane]
    forward_x[KX : KX + HALF, :GRID] = -sin[:HALF][:, plane]
    weight = np.where((k[:HALF] == 0) | (k[:HALF] == GRID // 2), 1.0, 2.0) / GRID**3
    inverse_x = np.zeros((XR, 2 * KX))
    inverse_x[:GRID, :HALF] = (weight[:, None] * cos[:HALF][:, plane]).T
    inverse_x[:GRID, KX : KX + HALF] = -(weight[:, None] * sin[:HALF][:, plane]).T
    along_z = np.zeros((LANES, 2 * LANES))
    along_z[:GRID, :GRID] = cos
    along_z[:GRID, LANES : LANES + GRID] = sin
    forward_y = np.block([[cos, sin], [-sin, cos]])
    inverse_y = np.block([[cos, -sin], [sin, cos]])

    def left(table):
        high, low = split_np(table)
        return np.concatenate([high, high, low], axis=1)

    z_high, z_low = split_np(along_z)
    z_three = np.concatenate([z_high, z_high, z_low], axis=0)
    fold = np.where(k > GRID // 2, k - GRID, k).astype(np.float64)
    squares = np.ones((GRID, LANES))
    squares[:, :GRID] = fold[:, None] ** 2 + fold[None, :] ** 2
    return (
        left(forward_x),
        left(inverse_x),
        z_three,
        left(forward_y),
        left(inverse_y),
        squares.astype(np.float32),
    )


def split(x):
    high = x.astype(BF16)
    low = (x - high.astype(F32)).astype(BF16)
    return high, low


def left_dot(table, x):
    high, low = split(x)
    return jnp.dot(table, jnp.concatenate([high, low, high], axis=0), preferred_element_type=F32)


def right_dot(x, table):
    high, low = split(x)
    three = jnp.concatenate([high, low, high], axis=1)
    return jnp.dot(three, table, preferred_element_type=F32)


def pick(index, choices):
    value = choices[0]
    for d in range(1, len(choices)):
        value = jnp.where(index == d, choices[d], value)
    return value


def shape(*dims):
    return jax.ShapeDtypeStruct(dims, F32)


def call(kernel, out_shape, owner, *arrays, after=(), scratch=(), flops=0, vmem=8):
    specs = [pl.BlockSpec(memory_space=pltpu.SMEM)]
    specs += [pl.BlockSpec(memory_space=pltpu.VMEM) for _ in arrays]
    specs += [pl.BlockSpec(memory_space=pl.ANY) for _ in after]
    size = sum(a.size for a in arrays) * 4

    def body(owner_ref, *refs):
        kernel(scalars(owner_ref), *refs)

    return pl.pallas_call(
        body,
        in_specs=specs,
        out_shape=out_shape,
        scratch_shapes=list(scratch),
        compiler_params=pltpu.CompilerParams(vmem_limit_bytes=vmem * 2**20),
        cost_estimate=pl.CostEstimate(flops=flops, bytes_accessed=2 * size, transcendentals=0),
    )(owner, *arrays, *after)


MY_X, MY_C, MY_Z, X_STEP, C_OWN, Z_STEP, MY_Y, MY_PAIR = 0, 1, 2, 3, 5, 7, 9, 10


def divide_grid():
    me = lax.axis_index("grid")
    return me // 2, lax.rem(me, 2)


def scalars(owner):
    me = lax.axis_index("band")
    x, c, z = lax.rem(me // 2, 4), lax.rem(me, 2), me // 8
    values = [x, c, z, 0, 0, 0, 0, 0, 0, *divide_grid()]
    for step in range(2):
        band = jnp.clip(owner[step], 0, BAND - 1)
        values[X_STEP + step] = lax.rem(x + 4 - lax.rem(band // 2, 4), 4)
        values[C_OWN + step] = (c == lax.rem(band, 2)).astype(jnp.int32)
        values[Z_STEP + step] = lax.rem(z + 4 - band // 8, 4)
    return values


def pack_kernel(info, orb_ref, stay_ref, cross_ref, q0, q1, q2, q3, out_ref):
    for o in range(2):
        out_ref[o, TAIL:ROWS, :] = jnp.zeros((ROWS - TAIL, LANES), F32)
        for t in range(TILES):
            wide = min(LANES, PLANE - t * LANES)
            if wide < LANES:
                out_ref[o, 8 * t : 8 * t + 8, :] = jnp.zeros((8, LANES), F32)
            cols = slice(t * LANES, t * LANES + wide)
            out_ref[o, 8 * t : 8 * t + 8, :wide] = orb_ref[o, 0:8, cols]
            out_ref[o, TAIL + t : TAIL + t + 1, :wide] = orb_ref[o, 8:9, cols]
    stay_ref[...] = out_ref[info[MY_PAIR]]
    cross_ref[...] = out_ref[1 - info[MY_PAIR]]
    for d, quarter in enumerate((q0, q1, q2, q3)):
        first = pl.multiple_of(QUARTER * lax.rem(info[MY_X] + d, 4), QUARTER)
        for o in range(2):
            quarter[o] = out_ref[o, pl.ds(first, QUARTER), :]


def join_kernel(info, stay_ref, got_ref, out_ref):
    out_ref[0] = stay_ref[...]
    out_ref[1] = got_ref[...]


def pick_x_kernel(info, q0, q1, q2, q3, keep_ref, give_ref):
    for ref, half in ((keep_ref, info[MY_C]), (give_ref, 1 - info[MY_C])):
        rows = pl.ds(pl.multiple_of(half * PIECE, PIECE), PIECE)
        for step in range(2):
            for m in range(2):
                choices = [q[m, rows, :] for q in (q0, q1, q2, q3)]
                ref[2 * step + m] = pick(info[X_STEP + step], choices)


def pick_core_kernel(info, keep_ref, got_ref, out_ref):
    for b in range(4):
        out_ref[b] = jnp.where(info[C_OWN + b // 2] == 1, keep_ref[b], got_ref[b])


def pick_z_kernel(info, z0, z1, z2, z3, out_ref):
    for b in range(4):
        value = pick(info[Z_STEP + b // 2], [z[b] for z in (z0, z1, z2, z3)])
        out_ref[2 * b] = value
        out_ref[2 * b + 1] = value


def whole(r, info, scale):
    for d in range(4):
        y = lax.rem(info[MY_Y] + 4 - d, 4)
        r.orb[2 * y + info[MY_PAIR]] = r.slabs[d][0]
        r.orb[2 * y + 1 - info[MY_PAIR]] = r.slabs[d][1]
    for d in range(4):
        quarter = QUARTER * lax.rem(info[MY_X] + 4 - d, 4)
        for ref, half in ((r.mine[d], info[MY_C]), (r.other[d], 1 - info[MY_C])):
            rows = pl.ds(pl.multiple_of(quarter + PIECE * half, PIECE), PIECE)
            for s in range(8):
                r.blk[s, rows, :] = ref[s]


def density(r, info, scale):
    r.wide[GRID:XR, :] = jnp.zeros((XR - GRID, (TILES + 2) * LANES), F32)
    for t in range(TILES):
        cols = slice(t * LANES, (t + 1) * LANES)
        rows = slice(8 * t, 8 * t + 8)
        for s in range(8):
            r.wide[8 * s : 8 * s + 8, cols] = r.orb[s, rows, :] * r.blk[s, rows, :]
            r.orb_tail[s : s + 1, cols] = r.orb[s, TAIL + t : TAIL + t + 1, :]
            r.blk_tail[s : s + 1, cols] = r.blk[s, TAIL + t : TAIL + t + 1, :]
        r.wide[64:72, cols] = r.orb_tail[:, cols] * r.blk_tail[:, cols]


def forward_x(r, info, scale):
    for t in range(0, TILES, 4):
        cols = slice(t * LANES, min(t + 4, TILES) * LANES)
        r.wide[:, cols] = left_dot(r.fx[...], r.wide[:, cols])


def to_columns(r, info, scale):
    lane = lax.broadcasted_iota(jnp.int32, (XR, LANES), 1)
    for y in range(GRID):
        t, off = divmod(y * GRID, LANES)
        value = r.wide[:, t * LANES : (t + 1) * LANES]
        if off:
            value = pltpu.roll(value, LANES - off, 1)
            if off + GRID > LANES:
                after = pltpu.roll(r.wide[:, (t + 1) * LANES : (t + 2) * LANES], LANES - off, 1)
                value = jnp.where(lane < LANES - off, value, after)
        r.col[y * XR : (y + 1) * XR, :] = value


def forward_z(r, info, scale):
    def step(j, carry):
        base = pl.multiple_of(j * LINES * XR, LINES * XR)
        both = right_dot(r.col[pl.ds(base, LINES * XR), :], r.zt[...])
        base = pl.multiple_of(j * LINES * KX, LINES * KX)
        for y in range(LINES):
            real = both[y * XR : y * XR + KX]
            imag = both[y * XR + KX : (y + 1) * XR]
            rows = pl.ds(base + y * KX, KX)
            r.re[rows, :] = real[:, :LANES] + imag[:, LANES:]
            r.im[rows, :] = imag[:, :LANES] - real[:, LANES:]
        return carry

    lax.fori_loop(0, GRID // LINES, step, 0)


def along_y(r, info, scale):
    def step(j, carry):
        strides = [pl.ds(GROUP * j + q, GRID, stride=KX) for q in range(GROUP)]
        lines = [jnp.concatenate([r.re[s, :], r.im[s, :]], axis=0) for s in strides]
        spec = left_dot(r.fy[...], jnp.concatenate(lines, axis=1))
        factors = []
        for q in range(GROUP):
            kx = (GROUP * j + q).astype(F32)
            square = r.sq[...] + kx * kx
            factor = jnp.where(square > 0, scale / jnp.maximum(square, 1.0), 0.0)
            factors.append(jnp.concatenate([factor, factor], axis=0))
        spec = spec * jnp.concatenate(factors, axis=1)
        back = left_dot(r.iy[...], spec)
        for q, s in enumerate(strides):
            cols = slice(q * LANES, (q + 1) * LANES)
            r.re[s, :] = back[:GRID, cols]
            r.im[s, :] = back[GRID:, cols]
        return carry

    lax.fori_loop(0, KX // GROUP, step, 0)


def inverse_z(r, info, scale):
    def step(j, carry):
        base = pl.multiple_of(j * LINES * KX, LINES * KX)
        rows = pl.ds(base, LINES * KX)
        real = right_dot(r.re[rows, :], r.zt[...])
        imag = right_dot(r.im[rows, :], r.zt[...])
        new_re = real[:, :LANES] - imag[:, LANES:]
        new_im = real[:, LANES:] + imag[:, :LANES]
        base = pl.multiple_of(j * LINES * XR, LINES * XR)
        for y in range(LINES):
            r.col[pl.ds(base + y * XR, KX), :] = new_re[y * KX : (y + 1) * KX]
            r.col[pl.ds(base + y * XR + KX, KX), :] = new_im[y * KX : (y + 1) * KX]
        return carry

    lax.fori_loop(0, GRID // LINES, step, 0)


def from_columns(r, info, scale):
    lane = lax.broadcasted_iota(jnp.int32, (XR, LANES), 1)
    for t in range(TILES):
        value = jnp.zeros((XR, LANES), F32)
        for y in range(GRID):
            at = y * GRID - t * LANES
            if at >= LANES or at + GRID <= 0:
                continue
            piece = r.col[y * XR : (y + 1) * XR, :]
            if at % LANES:
                piece = pltpu.roll(piece, at % LANES, 1)
            keep = (lane >= at) & (lane < at + GRID)
            value = jnp.where(keep, piece, value)
        r.wide[:, t * LANES : (t + 1) * LANES] = value


def inverse_x(r, info, scale):
    for s in range(8):
        r.own[s, TAIL + TILES : ROWS, :] = jnp.zeros((ROWS - TAIL - TILES, LANES), F32)
    for t in range(0, TILES, 4):
        last = min(t + 4, TILES)
        cols = slice(t * LANES, last * LANES)
        pot = -left_dot(r.ix[...], r.wide[:, cols])
        for u in range(t, last):
            part = pot[:, (u - t) * LANES : (u - t + 1) * LANES]
            rows = slice(8 * u, 8 * u + 8)
            one = slice(u * LANES, (u + 1) * LANES)
            tail = part[64:72] * r.blk_tail[:, one]
            for s in range(8):
                piece = part[8 * s : 8 * s + 8]
                r.own[s, rows, :] = piece * r.blk[s, rows, :]
                r.own[s, TAIL + u : TAIL + u + 1, :] = tail[s : s + 1]
                r.wide[8 * s : 8 * s + 8, one] = piece * r.orb[s, rows, :]
            r.wide[64:72, one] = part[64:72] * r.orb_tail[:, one]
    r.wide[:, TILES * LANES :] = jnp.zeros((XR, 2 * LANES), F32)
    for d in range(4):
        y = lax.rem(info[MY_Y] + d, 4)
        r.sent[d][0] = r.own[2 * y + info[MY_PAIR]]
        r.sent[d][1] = r.own[2 * y + 1 - info[MY_PAIR]]


def share_out(r, info, scale):
    lane = lax.broadcasted_iota(jnp.int32, (GRID, LANES), 1)
    third = lane[:8]

    def turned(tile, turn):
        value = r.wide[:GRID, tile * LANES : (tile + 1) * LANES]
        return pltpu.roll(value, turn, 1) if turn else value

    for band in range(BAND):
        z, x, c = band // 8, band // 2 % 4, band % 2
        core = lax.rem(c + info[MY_C], 2)
        place = 4 * core + lax.rem(x + 4 - info[MY_X], 4)
        z = lax.rem(z + 4 - info[MY_Z], 4)
        t, off = divmod(band * SHARE, LANES)
        turn = (LANES - off) % LANES
        first, second = turned(t, turn), turned(t + 1, turn)
        head, rest = jnp.where(lane < LANES - off, first, second), second
        if off + REST > LANES:
            rest = jnp.where(lane < LANES - off, second, turned(t + 2, turn))
        r.cut[place, z, :GRID, :] = head
        for j in range(3):
            one, two, three = (rest[8 * (3 * j + k) : 8 * (3 * j + k) + 8] for k in range(3))
            two, three = pltpu.roll(two, REST, 1), pltpu.roll(three, 2 * REST, 1)
            packed = jnp.where(third < REST, one, jnp.where(third < 2 * REST, two, three))
            r.cut[place, z, GRID + 8 * j : GRID + 8 * j + 8, :] = packed
    for x in range(4):
        r.keep[x][...] = r.cut[x]
        r.give[x][...] = r.cut[4 + x]


STAGES = (
    whole,
    density,
    forward_x,
    to_columns,
    forward_z,
    along_y,
    inverse_z,
    from_columns,
    inverse_x,
    share_out,
)


def field_kernel(scale, info, *refs):
    tables = ("fx", "ix", "zt", "fy", "iy", "sq")
    scratch = ("orb", "blk", "own", "wide", "orb_tail", "blk_tail", "col", "re", "im", "cut")
    r = types.SimpleNamespace(slabs=refs[:4], mine=refs[4:8], other=refs[8:12])
    vars(r).update(zip(tables, refs[12:18]))
    r.sent, r.keep, r.give = refs[18:22], refs[22:26], refs[26:30]
    vars(r).update(zip(scratch, refs[30:]))
    for stage in STAGES:
        stage(r, info, scale)


def fields(block_owner, slabs, pieces, scale):
    def body(*refs):
        field_kernel(scale, *refs)

    whole_slabs = pltpu.VMEM((8, ROWS, LANES), F32)
    return call(
        body,
        [shape(2, ROWS, LANES)] * 4 + [shape(4, PACK, LANES)] * 8,
        block_owner,
        *slabs,
        *pieces,
        *[jnp.asarray(t) for t in tables()],
        scratch=[
            whole_slabs,
            whole_slabs,
            whole_slabs,
            pltpu.VMEM((XR, (TILES + 2) * LANES), F32),
            pltpu.VMEM((8, TILES * LANES), F32),
            pltpu.VMEM((8, TILES * LANES), F32),
            pltpu.VMEM((GRID * XR, LANES), F32),
            pltpu.VMEM((GRID * KX, LANES), F32),
            pltpu.VMEM((GRID * KX, LANES), F32),
            pltpu.VMEM((8, 4, PACK, LANES), F32),
        ],
        flops=10**10,
        vmem=36,
    )


def add_kernel(info, a_ref, b_ref, out_ref):
    out_ref[...] = a_ref[...] + b_ref[...]


def add_x_kernel(info, k_ref, g_ref, r1, r2, r3, *outs):
    for z in range(4):
        outs[z][...] = k_ref[z] + g_ref[z] + r1[z] + r2[z] + r3[z]


def add_z_kernel(info, s_ref, r1, r2, r3, out_ref, sum_ref):
    sum_ref[...] = s_ref[...] + r1[...] + r2[...] + r3[...]
    out_ref[...] = jnp.zeros((8, PART, LANES), F32)

    def rest(tile):
        value = sum_ref[GRID + 8 * (tile // 3) : GRID + 8 * (tile // 3) + 8, :]
        turn = tile % 3 * REST
        return pltpu.roll(value, LANES - turn, 1) if turn else value

    last = rest(8)
    for s in range(8):
        out_ref[s, 0:8, :] = sum_ref[8 * s : 8 * s + 8, :]
        out_ref[s, 8:16, :] = rest(s)
        out_ref[s, 16:17, :] = sum_ref[64 + s : 65 + s, :]
        out_ref[s, 17:18, :] = last[s : s + 1]


def share_kernel(info, part_ref, out_ref):
    for b in range(4):
        total = part_ref[2 * b] + part_ref[2 * b + 1]
        at = (b // 2, b % 2)
        out_ref[at[0], at[1], 0:8, :LANES] = total[0:8]
        out_ref[at[0], at[1], 0:8, LANES:SHARE] = total[8:16, :REST]
        out_ref[at[0], at[1], 8:9, :LANES] = total[16:17]
        out_ref[at[0], at[1], 8:9, LANES:SHARE] = total[17:18, :REST]


def add_y_kernel(info, s_ref, r1, r2, r3, stay_ref, cross_ref):
    for j, ref in enumerate((stay_ref, cross_ref)):
        ref[...] = s_ref[j] + r1[j] + r2[j] + r3[j]


def own_kernel(info, stay_ref, got_ref, out_ref):
    for ref, i in ((stay_ref, info[MY_PAIR]), (got_ref, 1 - info[MY_PAIR])):
        for t in range(TILES):
            wide = min(LANES, PLANE - t * LANES)
            cols = slice(t * LANES, t * LANES + wide)
            out_ref[i, 0:8, cols] = ref[8 * t : 8 * t + 8, :wide]
            out_ref[i, 8:9, cols] = ref[TAIL + t : TAIL + t + 1, :wide]


def shift_x(d):
    return [(i, i // 8 * 8 + (i // 2 + d) % 4 * 2 + i % 2) for i in range(BAND)]


def shift_z(d):
    return [(i, (i + 8 * d) % BAND) for i in range(BAND)]


def shift_y(d):
    return [(i, (i + 2 * d) % 8) for i in range(8)]


def other_slab(x):
    return lax.ppermute(x, "grid", [(i, i ^ 1) for i in range(8)])


def other_core(x):
    return lax.ppermute(x, "band", [(i, i ^ 1) for i in range(BAND)])


def on_device(orbitals, block_owner):
    scale = math.sqrt(GRID**3 / (2 * BAND))
    slab = shape(ROWS, LANES)
    stay, cross, *quarters = call(
        pack_kernel,
        [slab, slab] + [shape(2, QUARTER, LANES)] * 4,
        block_owner,
        orbitals,
        scratch=[pltpu.VMEM((2, ROWS, LANES), F32)],
    )
    pair = call(join_kernel, shape(2, ROWS, LANES), block_owner, stay, other_slab(cross))
    slabs = [pair] + [lax.ppermute(pair, "grid", shift_y(d)) for d in (1, 2, 3)]

    quarters = quarters[:1] + [lax.ppermute(quarters[d], "band", shift_x(d)) for d in (1, 2, 3)]
    half = shape(4, PIECE, LANES)
    keep, give = call(pick_x_kernel, [half, half], block_owner, *quarters)
    mine = call(pick_core_kernel, half, block_owner, keep, other_core(give))
    along = [mine] + [lax.ppermute(mine, "band", shift_z(d)) for d in (1, 2, 3)]
    mine = call(pick_z_kernel, shape(8, PIECE, LANES), block_owner, *along)
    piece = lax.all_to_all(mine, "grid", 0, 0)
    pieces = [piece] + [lax.ppermute(piece, "band", shift_x(d)) for d in (1, 2, 3)]
    pieces = pieces + [other_core(p) for p in pieces]

    outs = fields(block_owner, slabs, pieces, scale)
    sent, shares = list(outs[:4]), outs[4:]
    sent = sent[:1] + [lax.ppermute(sent[d], "grid", shift_y(d)) for d in (1, 2, 3)]
    stay, cross = call(add_y_kernel, [slab, slab], block_owner, *sent)
    own = other_slab(cross)
    kept, got = shares[:4], [other_core(g) for g in shares[4:]]
    part = shape(4, PACK, LANES)
    moved = []
    for d in (1, 2, 3):
        moved.append(lax.ppermute(call(add_kernel, part, block_owner, kept[d], got[d]), "band", shift_x(d)))
    sums = call(add_x_kernel, [shape(PACK, LANES)] * 4, block_owner, kept[0], got[0], *moved)
    moved = [lax.ppermute(sums[d], "band", shift_z(d)) for d in (1, 2, 3)]
    slabs = call(
        add_z_kernel,
        shape(8, PART, LANES),
        block_owner,
        sums[0],
        *moved,
        scratch=[pltpu.VMEM((PACK, LANES), F32)],
    )
    block_field = call(
        share_kernel, shape(2, 2, SLAB, SHARE), block_owner, lax.all_to_all(slabs, "grid", 0, 0)
    )
    field = call(own_kernel, shape(2, SLAB, PLANE), block_owner, stay, own)
    return field, block_field


def solution(mesh):
    return jax.shard_map(
        on_device,
        mesh=mesh,
        in_specs=(P("band", "grid", None), P()),
        out_specs=(P("band", "grid", None), P(None, None, "grid", "band")),
        check_vma=False,
    )
```

```python
import math
import types

import jax
import jax.numpy as jnp
import numpy as np
from jax import lax
from jax.experimental import pallas as pl
from jax.experimental.pallas import tpu as pltpu
from jax.sharding import PartitionSpec as P

GRID = 72
HALF = GRID // 2 + 1
LINES = 72
GROUP = 20
KX = 40
PLANE = GRID * GRID
TILES = 41
LANES = 128
SLAB = 9
TAIL = 8 * TILES
ROWS = 384
XR = 80
BAND = 32
QUARTER = ROWS // 4
PIECE = ROWS // 8
SHARE = PLANE // BAND
REST = SHARE - LANES
PACK = 96
PART = 24
F32 = jnp.float32
BF16 = jnp.bfloat16


def split_np(table):
    high = table.astype(jnp.bfloat16)
    low = (table - high.astype(np.float64)).astype(jnp.bfloat16)
    return high, low


def tables():
    k = np.arange(GRID)
    ang = 2.0 * np.pi / GRID * ((k[:, None] * k[None, :]) % GRID)
    cos, sin = np.cos(ang), np.sin(ang)
    place = np.arange(GRID)
    plane = np.where(place < 64, SLAB * (place // 8) + place % 8, SLAB * (place - 64) + 8)
    forward_x = np.zeros((2 * KX, XR))
    forward_x[:HALF, :GRID] = cos[:HALF][:, plane]
    forward_x[KX : KX + HALF, :GRID] = -sin[:HALF][:, plane]
    weight = np.where((k[:HALF] == 0) | (k[:HALF] == GRID // 2), 1.0, 2.0) / GRID**3
    inverse_x = np.zeros((XR, 2 * KX))
    inverse_x[:GRID, :HALF] = (weight[:, None] * cos[:HALF][:, plane]).T
    inverse_x[:GRID, KX : KX + HALF] = -(weight[:, None] * sin[:HALF][:, plane]).T
    along_z = np.zeros((LANES, 2 * LANES))
    along_z[:GRID, :GRID] = cos
    along_z[:GRID, LANES : LANES + GRID] = sin
    forward_y = np.block([[cos, sin], [-sin, cos]])
    inverse_y = np.block([[cos, -sin], [sin, cos]])

    def left(table):
        high, low = split_np(table)
        return np.concatenate([high, high, low], axis=1)

    z_high, z_low = split_np(along_z)
    z_three = np.concatenate([z_high, z_high, z_low], axis=0)
    fold = np.where(k > GRID // 2, k - GRID, k).astype(np.float64)
    squares = np.ones((GRID, LANES))
    squares[:, :GRID] = fold[:, None] ** 2 + fold[None, :] ** 2
    return (
        left(forward_x),
        left(inverse_x),
        z_three,
        left(forward_y),
        left(inverse_y),
        squares.astype(np.float32),
    )


def split(x):
    high = x.astype(BF16)
    low = (x - high.astype(F32)).astype(BF16)
    return high, low


def left_dot(table, x):
    high, low = split(x)
    return jnp.dot(table, jnp.concatenate([high, low, high], axis=0), preferred_element_type=F32)


def right_dot(x, table):
    high, low = split(x)
    three = jnp.concatenate([high, low, high], axis=1)
    return jnp.dot(three, table, preferred_element_type=F32)


def pick(index, choices):
    value = choices[0]
    for d in range(1, len(choices)):
        value = jnp.where(index == d, choices[d], value)
    return value


def shape(*dims):
    return jax.ShapeDtypeStruct(dims, F32)


def call(kernel, out_shape, owner, *arrays, after=(), scratch=(), flops=0, vmem=8):
    specs = [pl.BlockSpec(memory_space=pltpu.SMEM)]
    specs += [pl.BlockSpec(memory_space=pltpu.VMEM) for _ in arrays]
    specs += [pl.BlockSpec(memory_space=pl.ANY) for _ in after]
    size = sum(a.size for a in arrays) * 4

    def body(owner_ref, *refs):
        kernel(scalars(owner_ref), *refs)

    return pl.pallas_call(
        body,
        in_specs=specs,
        out_shape=out_shape,
        scratch_shapes=list(scratch),
        compiler_params=pltpu.CompilerParams(vmem_limit_bytes=vmem * 2**20),
        cost_estimate=pl.CostEstimate(flops=flops, bytes_accessed=2 * size, transcendentals=0),
    )(owner, *arrays, *after)


MY_X, MY_C, MY_Z, X_STEP, C_OWN, Z_STEP, MY_Y, MY_PAIR = 0, 1, 2, 3, 5, 7, 9, 10


def divide_grid():
    me = lax.axis_index("grid")
    return me // 2, lax.rem(me, 2)


def scalars(owner):
    me = lax.axis_index("band")
    x, c, z = lax.rem(me // 2, 4), lax.rem(me, 2), me // 8
    values = [x, c, z, 0, 0, 0, 0, 0, 0, *divide_grid()]
    for step in range(2):
        band = jnp.clip(owner[step], 0, BAND - 1)
        values[X_STEP + step] = lax.rem(x + 4 - lax.rem(band // 2, 4), 4)
        values[C_OWN + step] = (c == lax.rem(band, 2)).astype(jnp.int32)
        values[Z_STEP + step] = lax.rem(z + 4 - band // 8, 4)
    return values


def pack_kernel(info, orb_ref, stay_ref, cross_ref, q0, q1, q2, q3, out_ref):
    for o in range(2):
        out_ref[o, TAIL:ROWS, :] = jnp.zeros((ROWS - TAIL, LANES), F32)
        for t in range(TILES):
            wide = min(LANES, PLANE - t * LANES)
            if wide < LANES:
                out_ref[o, 8 * t : 8 * t + 8, :] = jnp.zeros((8, LANES), F32)
            cols = slice(t * LANES, t * LANES + wide)
            out_ref[o, 8 * t : 8 * t + 8, :wide] = orb_ref[o, 0:8, cols]
            out_ref[o, TAIL + t : TAIL + t + 1, :wide] = orb_ref[o, 8:9, cols]
    stay_ref[...] = out_ref[info[MY_PAIR]]
    cross_ref[...] = out_ref[1 - info[MY_PAIR]]
    for d, quarter in enumerate((q0, q1, q2, q3)):
        first = pl.multiple_of(QUARTER * lax.rem(info[MY_X] + d, 4), QUARTER)
        for o in range(2):
            quarter[o] = out_ref[o, pl.ds(first, QUARTER), :]


def join_kernel(info, stay_ref, got_ref, out_ref):
    out_ref[0] = stay_ref[...]
    out_ref[1] = got_ref[...]


def pick_x_kernel(info, q0, q1, q2, q3, keep_ref, give_ref):
    for ref, half in ((keep_ref, info[MY_C]), (give_ref, 1 - info[MY_C])):
        rows = pl.ds(pl.multiple_of(half * PIECE, PIECE), PIECE)
        for step in range(2):
            for m in range(2):
                choices = [q[m, rows, :] for q in (q0, q1, q2, q3)]
                ref[2 * step + m] = pick(info[X_STEP + step], choices)


def pick_core_kernel(info, keep_ref, got_ref, out_ref):
    for b in range(4):
        out_ref[b] = jnp.where(info[C_OWN + b // 2] == 1, keep_ref[b], got_ref[b])


def pick_z_kernel(info, z0, z1, z2, z3, *refs):
    out_ref = refs[-1]
    for b in range(4):
        value = pick(info[Z_STEP + b // 2], [z[b] for z in (z0, z1, z2, z3)])
        out_ref[2 * b] = value
        out_ref[2 * b + 1] = value


def whole(r, info, scale):
    for d in range(4):
        y = lax.rem(info[MY_Y] + 4 - d, 4)
        r.orb[2 * y + info[MY_PAIR]] = r.slabs[d][0]
        r.orb[2 * y + 1 - info[MY_PAIR]] = r.slabs[d][1]
    for d in range(4):
        quarter = QUARTER * lax.rem(info[MY_X] + 4 - d, 4)
        for ref, half in ((r.mine[d], info[MY_C]), (r.other[d], 1 - info[MY_C])):
            rows = pl.ds(pl.multiple_of(quarter + PIECE * half, PIECE), PIECE)
            for s in range(8):
                r.blk[s, rows, :] = ref[s]


def density(r, info, scale):
    r.wide[GRID:XR, :] = jnp.zeros((XR - GRID, (TILES + 2) * LANES), F32)
    for t in range(TILES):
        cols = slice(t * LANES, (t + 1) * LANES)
        rows = slice(8 * t, 8 * t + 8)
        for s in range(8):
            r.wide[8 * s : 8 * s + 8, cols] = r.orb[s, rows, :] * r.blk[s, rows, :]
            r.orb_tail[s : s + 1, cols] = r.orb[s, TAIL + t : TAIL + t + 1, :]
            r.blk_tail[s : s + 1, cols] = r.blk[s, TAIL + t : TAIL + t + 1, :]
        r.wide[64:72, cols] = r.orb_tail[:, cols] * r.blk_tail[:, cols]


def forward_x(r, info, scale):
    for t in range(0, TILES, 4):
        cols = slice(t * LANES, min(t + 4, TILES) * LANES)
        r.wide[:, cols] = left_dot(r.fx[...], r.wide[:, cols])


def to_columns(r, info, scale):
    lane = lax.broadcasted_iota(jnp.int32, (XR, LANES), 1)
    for y in range(GRID):
        t, off = divmod(y * GRID, LANES)
        value = r.wide[:, t * LANES : (t + 1) * LANES]
        if off:
            value = pltpu.roll(value, LANES - off, 1)
            if off + GRID > LANES:
                after = pltpu.roll(r.wide[:, (t + 1) * LANES : (t + 2) * LANES], LANES - off, 1)
                value = jnp.where(lane < LANES - off, value, after)
        r.col[y * XR : (y + 1) * XR, :] = value


def forward_z(r, info, scale):
    def step(j, carry):
        base = pl.multiple_of(j * LINES * XR, LINES * XR)
        both = right_dot(r.col[pl.ds(base, LINES * XR), :], r.zt[...])
        base = pl.multiple_of(j * LINES * KX, LINES * KX)
        for y in range(LINES):
            real = both[y * XR : y * XR + KX]
            imag = both[y * XR + KX : (y + 1) * XR]
            rows = pl.ds(base + y * KX, KX)
            r.re[rows, :] = real[:, :LANES] + imag[:, LANES:]
            r.im[rows, :] = imag[:, :LANES] - real[:, LANES:]
        return carry

    lax.fori_loop(0, GRID // LINES, step, 0)


def along_y(r, info, scale):
    def step(j, carry):
        strides = [pl.ds(GROUP * j + q, GRID, stride=KX) for q in range(GROUP)]
        lines = [jnp.concatenate([r.re[s, :], r.im[s, :]], axis=0) for s in strides]
        spec = left_dot(r.fy[...], jnp.concatenate(lines, axis=1))
        factors = []
        for q in range(GROUP):
            kx = (GROUP * j + q).astype(F32)
            square = r.sq[...] + kx * kx
            factor = jnp.where(square > 0, scale / jnp.maximum(square, 1.0), 0.0)
            factors.append(jnp.concatenate([factor, factor], axis=0))
        spec = spec * jnp.concatenate(factors, axis=1)
        back = left_dot(r.iy[...], spec)
        for q, s in enumerate(strides):
            cols = slice(q * LANES, (q + 1) * LANES)
            r.re[s, :] = back[:GRID, cols]
            r.im[s, :] = back[GRID:, cols]
        return carry

    lax.fori_loop(0, KX // GROUP, step, 0)


def inverse_z(r, info, scale):
    def step(j, carry):
        base = pl.multiple_of(j * LINES * KX, LINES * KX)
        rows = pl.ds(base, LINES * KX)
        real = right_dot(r.re[rows, :], r.zt[...])
        imag = right_dot(r.im[rows, :], r.zt[...])
        new_re = real[:, :LANES] - imag[:, LANES:]
        new_im = real[:, LANES:] + imag[:, :LANES]
        base = pl.multiple_of(j * LINES * XR, LINES * XR)
        for y in range(LINES):
            r.col[pl.ds(base + y * XR, KX), :] = new_re[y * KX : (y + 1) * KX]
            r.col[pl.ds(base + y * XR + KX, KX), :] = new_im[y * KX : (y + 1) * KX]
        return carry

    lax.fori_loop(0, GRID // LINES, step, 0)


def from_columns(r, info, scale):
    lane = lax.broadcasted_iota(jnp.int32, (XR, LANES), 1)
    for t in range(TILES):
        value = jnp.zeros((XR, LANES), F32)
        for y in range(GRID):
            at = y * GRID - t * LANES
            if at >= LANES or at + GRID <= 0:
                continue
            piece = r.col[y * XR : (y + 1) * XR, :]
            if at % LANES:
                piece = pltpu.roll(piece, at % LANES, 1)
            keep = (lane >= at) & (lane < at + GRID)
            value = jnp.where(keep, piece, value)
        r.wide[:, t * LANES : (t + 1) * LANES] = value


def inverse_x(r, info, scale):
    for s in range(8):
        r.own[s, TAIL + TILES : ROWS, :] = jnp.zeros((ROWS - TAIL - TILES, LANES), F32)
    for t in range(0, TILES, 4):
        last = min(t + 4, TILES)
        cols = slice(t * LANES, last * LANES)
        pot = -left_dot(r.ix[...], r.wide[:, cols])
        for u in range(t, last):
            part = pot[:, (u - t) * LANES : (u - t + 1) * LANES]
            rows = slice(8 * u, 8 * u + 8)
            one = slice(u * LANES, (u + 1) * LANES)
            tail = part[64:72] * r.blk_tail[:, one]
            for s in range(8):
                piece = part[8 * s : 8 * s + 8]
                r.own[s, rows, :] = piece * r.blk[s, rows, :]
                r.own[s, TAIL + u : TAIL + u + 1, :] = tail[s : s + 1]
                r.wide[8 * s : 8 * s + 8, one] = piece * r.orb[s, rows, :]
            r.wide[64:72, one] = part[64:72] * r.orb_tail[:, one]
    r.wide[:, TILES * LANES :] = jnp.zeros((XR, 2 * LANES), F32)


def share_out(r, info, scale):
    lane = lax.broadcasted_iota(jnp.int32, (GRID, LANES), 1)
    third = lane[:8]

    def turned(tile, turn):
        value = r.wide[:GRID, tile * LANES : (tile + 1) * LANES]
        return pltpu.roll(value, turn, 1) if turn else value

    for band in range(BAND):
        z, x, c = band // 8, band // 2 % 4, band % 2
        core = lax.rem(c + info[MY_C], 2)
        place = 4 * core + lax.rem(x + 4 - info[MY_X], 4)
        z = lax.rem(z + 4 - info[MY_Z], 4)
        t, off = divmod(band * SHARE, LANES)
        turn = (LANES - off) % LANES
        first, second = turned(t, turn), turned(t + 1, turn)
        head, rest = jnp.where(lane < LANES - off, first, second), second
        if off + REST > LANES:
            rest = jnp.where(lane < LANES - off, second, turned(t + 2, turn))
        r.cut[place, z, :GRID, :] = head
        for j in range(3):
            one, two, three = (rest[8 * (3 * j + k) : 8 * (3 * j + k) + 8] for k in range(3))
            two, three = pltpu.roll(two, REST, 1), pltpu.roll(three, 2 * REST, 1)
            packed = jnp.where(third < REST, one, jnp.where(third < 2 * REST, two, three))
            r.cut[place, z, GRID + 8 * j : GRID + 8 * j + 8, :] = packed
    for x in range(4):
        r.keep[x][...] = r.cut[x]
        r.give[x][...] = r.cut[4 + x]


STAGES = (
    whole,
    density,
    forward_x,
    to_columns,
    forward_z,
    along_y,
    inverse_z,
    from_columns,
    inverse_x,
    share_out,
)


def field_kernel(scale, info, *refs):
    tables = ("fx", "ix", "zt", "fy", "iy", "sq")
    scratch = ("orb", "blk", "wide", "orb_tail", "blk_tail", "col", "re", "im", "cut")
    r = types.SimpleNamespace(slabs=refs[:4], mine=refs[4:8], other=refs[8:12])
    vars(r).update(zip(tables, refs[12:18]))
    r.own, r.keep, r.give = refs[18], refs[19:23], refs[23:27]
    vars(r).update(zip(scratch, refs[27:]))
    for stage in STAGES:
        stage(r, info, scale)


def fields(block_owner, slabs, pieces, scale):
    def body(*refs):
        field_kernel(scale, *refs)

    whole_slabs = pltpu.VMEM((8, ROWS, LANES), F32)
    return call(
        body,
        [shape(8, ROWS, LANES)] + [shape(4, PACK, LANES)] * 8,
        block_owner,
        *slabs,
        *pieces,
        *[jnp.asarray(t) for t in tables()],
        scratch=[
            whole_slabs,
            whole_slabs,
            pltpu.VMEM((XR, (TILES + 2) * LANES), F32),
            pltpu.VMEM((8, TILES * LANES), F32),
            pltpu.VMEM((8, TILES * LANES), F32),
            pltpu.VMEM((GRID * XR, LANES), F32),
            pltpu.VMEM((GRID * KX, LANES), F32),
            pltpu.VMEM((GRID * KX, LANES), F32),
            pltpu.VMEM((8, 4, PACK, LANES), F32),
        ],
        flops=10**10,
        vmem=36,
    )


def send_kernel(info, own_ref, after_ref, *outs):
    for d in range(4):
        y = lax.rem(info[MY_Y] + d, 4)
        outs[d][0] = own_ref[2 * y + info[MY_PAIR]]
        outs[d][1] = own_ref[2 * y + 1 - info[MY_PAIR]]


def add_core_kernel(info, *refs):
    for d in range(3):
        refs[6 + d][...] = refs[d][...] + refs[3 + d][...]


def add_x_kernel(info, k_ref, g_ref, r1, r2, r3, *outs):
    for z in range(4):
        outs[z][...] = k_ref[z] + g_ref[z] + r1[z] + r2[z] + r3[z]


def add_z_kernel(info, s_ref, r1, r2, r3, out_ref, sum_ref):
    sum_ref[...] = s_ref[...] + r1[...] + r2[...] + r3[...]
    out_ref[...] = jnp.zeros((8, PART, LANES), F32)

    def rest(tile):
        value = sum_ref[GRID + 8 * (tile // 3) : GRID + 8 * (tile // 3) + 8, :]
        turn = tile % 3 * REST
        return pltpu.roll(value, LANES - turn, 1) if turn else value

    last = rest(8)
    for s in range(8):
        out_ref[s, 0:8, :] = sum_ref[8 * s : 8 * s + 8, :]
        out_ref[s, 8:16, :] = rest(s)
        out_ref[s, 16:17, :] = sum_ref[64 + s : 65 + s, :]
        out_ref[s, 17:18, :] = last[s : s + 1]


def share_kernel(info, part_ref, after_ref, out_ref):
    for b in range(4):
        total = part_ref[2 * b] + part_ref[2 * b + 1]
        at = (b // 2, b % 2)
        out_ref[at[0], at[1], 0:8, :LANES] = total[0:8]
        out_ref[at[0], at[1], 0:8, LANES:SHARE] = total[8:16, :REST]
        out_ref[at[0], at[1], 8:9, :LANES] = total[16:17]
        out_ref[at[0], at[1], 8:9, LANES:SHARE] = total[17:18, :REST]


def add_y_kernel(info, s_ref, r1, r2, r3, after_ref, stay_ref, cross_ref):
    for j, ref in enumerate((stay_ref, cross_ref)):
        ref[...] = s_ref[j] + r1[j] + r2[j] + r3[j]


def own_kernel(info, stay_ref, got_ref, out_ref):
    for ref, i in ((stay_ref, info[MY_PAIR]), (got_ref, 1 - info[MY_PAIR])):
        for t in range(TILES):
            wide = min(LANES, PLANE - t * LANES)
            cols = slice(t * LANES, t * LANES + wide)
            out_ref[i, 0:8, cols] = ref[8 * t : 8 * t + 8, :wide]
            out_ref[i, 8:9, cols] = ref[TAIL + t : TAIL + t + 1, :wide]


def shift_x(d):
    return [(i, i // 8 * 8 + (i // 2 + d) % 4 * 2 + i % 2) for i in range(BAND)]


def shift_z(d):
    return [(i, (i + 8 * d) % BAND) for i in range(BAND)]


def shift_y(d):
    return [(i, (i + 2 * d) % 8) for i in range(8)]


def other_slab(x):
    return lax.ppermute(x, "grid", [(i, i ^ 1) for i in range(8)])


def other_core(x):
    return lax.ppermute(x, "band", [(i, i ^ 1) for i in range(BAND)])


def on_device(orbitals, block_owner):
    scale = math.sqrt(GRID**3 / (2 * BAND))
    slab = shape(ROWS, LANES)
    stay, cross, *quarters = call(
        pack_kernel,
        [slab, slab] + [shape(2, QUARTER, LANES)] * 4,
        block_owner,
        orbitals,
        scratch=[pltpu.VMEM((2, ROWS, LANES), F32)],
    )
    pair = call(join_kernel, shape(2, ROWS, LANES), block_owner, stay, other_slab(cross))
    slabs = [pair] + [lax.ppermute(pair, "grid", shift_y(d)) for d in (1, 3)]
    slabs.insert(2, lax.ppermute(slabs[1], "grid", shift_y(1)))

    quarters = quarters[:1] + [lax.ppermute(quarters[d], "band", shift_x(d)) for d in (1, 2, 3)]
    half = shape(4, PIECE, LANES)
    keep, give = call(pick_x_kernel, [half, half], block_owner, *quarters)
    mine = call(pick_core_kernel, half, block_owner, keep, other_core(give))
    along = [mine] + [lax.ppermute(mine, "band", shift_z(d)) for d in (1, 2, 3)]
    mine = call(pick_z_kernel, shape(8, PIECE, LANES), block_owner, *along)
    piece = lax.all_to_all(mine, "grid", 0, 0)
    pieces = [piece] + [lax.ppermute(piece, "band", shift_x(d)) for d in (1, 2, 3)]
    pieces = pieces + [other_core(p) for p in pieces]

    own, *shares = fields(block_owner, slabs, pieces, scale)
    kept, got = shares[:4], [other_core(g) for g in shares[4:]]
    part = shape(4, PACK, LANES)
    added = call(add_core_kernel, [part] * 3, block_owner, *kept[1:], *got[1:])
    moved = [lax.ppermute(added[d - 1], "band", shift_x(d)) for d in (1, 2, 3)]
    sent = call(send_kernel, [shape(2, ROWS, LANES)] * 4, block_owner, own, after=added[:1])
    sent = [sent[0]] + [lax.ppermute(sent[d], "grid", shift_y(d)) for d in (1, 2, 3)]
    sums = call(add_x_kernel, [shape(PACK, LANES)] * 4, block_owner, kept[0], got[0], *moved)
    moved = [lax.ppermute(sums[d], "band", shift_z(d)) for d in (1, 2, 3)]
    slabs = call(
        add_z_kernel,
        shape(8, PART, LANES),
        block_owner,
        sums[0],
        *moved,
        scratch=[pltpu.VMEM((PACK, LANES), F32)],
    )
    stay, cross = call(add_y_kernel, [slab, slab], block_owner, *sent, after=[slabs])
    field = call(own_kernel, shape(2, SLAB, PLANE), block_owner, stay, other_slab(cross))
    slabs = lax.all_to_all(slabs, "grid", 0, 0)
    block_field = call(
        share_kernel, shape(2, 2, SLAB, SHARE), block_owner, slabs, after=[field]
    )
    return field, block_field


def solution(mesh):
    return jax.shard_map(
        on_device,
        mesh=mesh,
        in_specs=(P("band", "grid", None), P()),
        out_specs=(P("band", "grid", None), P(None, None, "grid", "band")),
        check_vma=False,
    )
```

```python
import math
import types

import jax
import jax.numpy as jnp
import numpy as np
from jax import lax
from jax.experimental import pallas as pl
from jax.experimental.pallas import tpu as pltpu
from jax.sharding import PartitionSpec as P

GRID = 72
HALF = GRID // 2 + 1
LINES = 72
GROUP = 20
KX = 40
PLANE = GRID * GRID
TILES = 41
LANES = 128
SLAB = 9
TAIL = 8 * TILES
ROWS = 384
XR = 80
BAND = 32
QUARTER = ROWS // 4
PIECE = ROWS // 8
SHARE = PLANE // BAND
REST = SHARE - LANES
PACK = 96
PART = 24
F32 = jnp.float32
BF16 = jnp.bfloat16


def split_np(table):
    high = table.astype(jnp.bfloat16)
    low = (table - high.astype(np.float64)).astype(jnp.bfloat16)
    return high, low


def tables():
    k = np.arange(GRID)
    ang = 2.0 * np.pi / GRID * ((k[:, None] * k[None, :]) % GRID)
    cos, sin = np.cos(ang), np.sin(ang)
    place = np.arange(GRID)
    plane = np.where(place < 64, SLAB * (place // 8) + place % 8, SLAB * (place - 64) + 8)
    forward_x = np.zeros((2 * KX, XR))
    forward_x[:HALF, :GRID] = cos[:HALF][:, plane]
    forward_x[KX : KX + HALF, :GRID] = -sin[:HALF][:, plane]
    weight = np.where((k[:HALF] == 0) | (k[:HALF] == GRID // 2), 1.0, 2.0) / GRID**3
    inverse_x = np.zeros((XR, 2 * KX))
    inverse_x[:GRID, :HALF] = (weight[:, None] * cos[:HALF][:, plane]).T
    inverse_x[:GRID, KX : KX + HALF] = -(weight[:, None] * sin[:HALF][:, plane]).T
    along_z = np.zeros((LANES, 2 * LANES))
    along_z[:GRID, :GRID] = cos
    along_z[:GRID, LANES : LANES + GRID] = sin
    forward_y = np.block([[cos, sin], [-sin, cos]])
    inverse_y = np.block([[cos, -sin], [sin, cos]])

    def left(table):
        high, low = split_np(table)
        return np.concatenate([high, high, low], axis=1)

    z_high, z_low = split_np(along_z)
    z_three = np.concatenate([z_high, z_high, z_low], axis=0)
    fold = np.where(k > GRID // 2, k - GRID, k).astype(np.float64)
    squares = np.ones((GRID, LANES))
    squares[:, :GRID] = fold[:, None] ** 2 + fold[None, :] ** 2
    return (
        left(forward_x),
        left(inverse_x),
        z_three,
        left(forward_y),
        left(inverse_y),
        squares.astype(np.float32),
    )


def split(x):
    high = x.astype(BF16)
    low = (x - high.astype(F32)).astype(BF16)
    return high, low


def left_dot(table, x):
    high, low = split(x)
    return jnp.dot(table, jnp.concatenate([high, low, high], axis=0), preferred_element_type=F32)


def right_dot(x, table):
    high, low = split(x)
    three = jnp.concatenate([high, low, high], axis=1)
    return jnp.dot(three, table, preferred_element_type=F32)


def pick(index, choices):
    value = choices[0]
    for d in range(1, len(choices)):
        value = jnp.where(index == d, choices[d], value)
    return value


def shape(*dims):
    return jax.ShapeDtypeStruct(dims, F32)


def call(kernel, out_shape, owner, *arrays, after=(), scratch=(), flops=0, vmem=8):
    specs = [pl.BlockSpec(memory_space=pltpu.VMEM) for _ in arrays]
    specs += [pl.BlockSpec(memory_space=pl.ANY) for _ in after]
    size = sum(a.size for a in arrays) * 4
    operands = [*arrays, *after]
    if owner is not None:
        specs = [pl.BlockSpec(memory_space=pltpu.SMEM)] + specs
        operands = [owner] + operands

    def body(*refs):
        if owner is None:
            kernel(scalars(), *refs)
        else:
            kernel(scalars(refs[0]), *refs[1:])

    return pl.pallas_call(
        body,
        in_specs=specs,
        out_shape=out_shape,
        scratch_shapes=list(scratch),
        compiler_params=pltpu.CompilerParams(vmem_limit_bytes=vmem * 2**20),
        cost_estimate=pl.CostEstimate(flops=flops, bytes_accessed=2 * size, transcendentals=0),
    )(*operands)


MY_X, MY_C, MY_Z, X_STEP, C_OWN, Z_STEP, MY_Y, MY_PAIR = 0, 1, 2, 3, 5, 7, 9, 10


def divide_grid():
    me = lax.axis_index("grid")
    return me // 2, lax.rem(me, 2)


def scalars(owner=None):
    me = lax.axis_index("band")
    x, c, z = lax.rem(me // 2, 4), lax.rem(me, 2), me // 8
    values = [x, c, z, 0, 0, 0, 0, 0, 0, *divide_grid()]
    for step in range(2 if owner is not None else 0):
        band = jnp.clip(owner[step], 0, BAND - 1)
        values[X_STEP + step] = lax.rem(x + 4 - lax.rem(band // 2, 4), 4)
        values[C_OWN + step] = (c == lax.rem(band, 2)).astype(jnp.int32)
        values[Z_STEP + step] = lax.rem(z + 4 - band // 8, 4)
    return values


def pack_kernel(info, orb_ref, stay_ref, cross_ref, q0, q1, q2, q3, out_ref):
    for o in range(2):
        out_ref[o, TAIL:ROWS, :] = jnp.zeros((ROWS - TAIL, LANES), F32)
        for t in range(TILES):
            wide = min(LANES, PLANE - t * LANES)
            if wide < LANES:
                out_ref[o, 8 * t : 8 * t + 8, :] = jnp.zeros((8, LANES), F32)
            cols = slice(t * LANES, t * LANES + wide)
            out_ref[o, 8 * t : 8 * t + 8, :wide] = orb_ref[o, 0:8, cols]
            out_ref[o, TAIL + t : TAIL + t + 1, :wide] = orb_ref[o, 8:9, cols]
    stay_ref[...] = out_ref[info[MY_PAIR]]
    cross_ref[...] = out_ref[1 - info[MY_PAIR]]
    for d, quarter in enumerate((q0, q1, q2, q3)):
        first = pl.multiple_of(QUARTER * lax.rem(info[MY_X] + d, 4), QUARTER)
        for o in range(2):
            quarter[o] = out_ref[o, pl.ds(first, QUARTER), :]


def join_kernel(info, stay_ref, got_ref, out_ref):
    out_ref[0] = stay_ref[...]
    out_ref[1] = got_ref[...]


def pick_x_kernel(info, q0, q1, q2, q3, keep_ref, give_ref):
    for ref, half in ((keep_ref, info[MY_C]), (give_ref, 1 - info[MY_C])):
        rows = pl.ds(pl.multiple_of(half * PIECE, PIECE), PIECE)
        for step in range(2):
            for m in range(2):
                choices = [q[m, rows, :] for q in (q0, q1, q2, q3)]
                ref[2 * step + m] = pick(info[X_STEP + step], choices)


def pick_core_kernel(info, keep_ref, got_ref, out_ref):
    for b in range(4):
        out_ref[b] = jnp.where(info[C_OWN + b // 2] == 1, keep_ref[b], got_ref[b])


def pick_z_kernel(info, z0, z1, z2, z3, *refs):
    out_ref = refs[-1]
    for b in range(4):
        value = pick(info[Z_STEP + b // 2], [z[b] for z in (z0, z1, z2, z3)])
        out_ref[2 * b] = value
        out_ref[2 * b + 1] = value


def whole(r, info, scale):
    for d in range(4):
        y = lax.rem(info[MY_Y] + 4 - d, 4)
        r.orb[2 * y + info[MY_PAIR]] = r.slabs[d][0]
        r.orb[2 * y + 1 - info[MY_PAIR]] = r.slabs[d][1]
    for d in range(4):
        quarter = QUARTER * lax.rem(info[MY_X] + 4 - d, 4)
        for ref, half in ((r.mine[d], info[MY_C]), (r.other[d], 1 - info[MY_C])):
            rows = pl.ds(pl.multiple_of(quarter + PIECE * half, PIECE), PIECE)
            for s in range(8):
                r.blk[s, rows, :] = ref[s]


def density(r, info, scale):
    r.wide[GRID:XR, :] = jnp.zeros((XR - GRID, (TILES + 2) * LANES), F32)
    for t in range(TILES):
        cols = slice(t * LANES, (t + 1) * LANES)
        rows = slice(8 * t, 8 * t + 8)
        for s in range(8):
            r.wide[8 * s : 8 * s + 8, cols] = r.orb[s, rows, :] * r.blk[s, rows, :]
            r.orb_tail[s : s + 1, cols] = r.orb[s, TAIL + t : TAIL + t + 1, :]
            r.blk_tail[s : s + 1, cols] = r.blk[s, TAIL + t : TAIL + t + 1, :]
        r.wide[64:72, cols] = r.orb_tail[:, cols] * r.blk_tail[:, cols]


def forward_x(r, info, scale):
    for t in range(0, TILES, 4):
        cols = slice(t * LANES, min(t + 4, TILES) * LANES)
        r.wide[:, cols] = left_dot(r.fx[...], r.wide[:, cols])


def to_columns(r, info, scale):
    lane = lax.broadcasted_iota(jnp.int32, (XR, LANES), 1)
    for y in range(GRID):
        t, off = divmod(y * GRID, LANES)
        value = r.wide[:, t * LANES : (t + 1) * LANES]
        if off:
            value = pltpu.roll(value, LANES - off, 1)
            if off + GRID > LANES:
                after = pltpu.roll(r.wide[:, (t + 1) * LANES : (t + 2) * LANES], LANES - off, 1)
                value = jnp.where(lane < LANES - off, value, after)
        r.col[y * XR : (y + 1) * XR, :] = value


def forward_z(r, info, scale):
    def step(j, carry):
        base = pl.multiple_of(j * LINES * XR, LINES * XR)
        both = right_dot(r.col[pl.ds(base, LINES * XR), :], r.zt[...])
        base = pl.multiple_of(j * LINES * KX, LINES * KX)
        for y in range(LINES):
            real = both[y * XR : y * XR + KX]
            imag = both[y * XR + KX : (y + 1) * XR]
            rows = pl.ds(base + y * KX, KX)
            r.re[rows, :] = real[:, :LANES] + imag[:, LANES:]
            r.im[rows, :] = imag[:, :LANES] - real[:, LANES:]
        return carry

    lax.fori_loop(0, GRID // LINES, step, 0)


def along_y(r, info, scale):
    def step(j, carry):
        strides = [pl.ds(GROUP * j + q, GRID, stride=KX) for q in range(GROUP)]
        lines = [jnp.concatenate([r.re[s, :], r.im[s, :]], axis=0) for s in strides]
        spec = left_dot(r.fy[...], jnp.concatenate(lines, axis=1))
        factors = []
        for q in range(GROUP):
            kx = (GROUP * j + q).astype(F32)
            square = r.sq[...] + kx * kx
            factor = jnp.where(square > 0, scale / jnp.maximum(square, 1.0), 0.0)
            factors.append(jnp.concatenate([factor, factor], axis=0))
        spec = spec * jnp.concatenate(factors, axis=1)
        back = left_dot(r.iy[...], spec)
        for q, s in enumerate(strides):
            cols = slice(q * LANES, (q + 1) * LANES)
            r.re[s, :] = back[:GRID, cols]
            r.im[s, :] = back[GRID:, cols]
        return carry

    lax.fori_loop(0, KX // GROUP, step, 0)


def inverse_z(r, info, scale):
    def step(j, carry):
        base = pl.multiple_of(j * LINES * KX, LINES * KX)
        rows = pl.ds(base, LINES * KX)
        real = right_dot(r.re[rows, :], r.zt[...])
        imag = right_dot(r.im[rows, :], r.zt[...])
        new_re = real[:, :LANES] - imag[:, LANES:]
        new_im = real[:, LANES:] + imag[:, :LANES]
        base = pl.multiple_of(j * LINES * XR, LINES * XR)
        for y in range(LINES):
            r.col[pl.ds(base + y * XR, KX), :] = new_re[y * KX : (y + 1) * KX]
            r.col[pl.ds(base + y * XR + KX, KX), :] = new_im[y * KX : (y + 1) * KX]
        return carry

    lax.fori_loop(0, GRID // LINES, step, 0)


def from_columns(r, info, scale):
    lane = lax.broadcasted_iota(jnp.int32, (XR, LANES), 1)
    for t in range(TILES):
        value = jnp.zeros((XR, LANES), F32)
        for y in range(GRID):
            at = y * GRID - t * LANES
            if at >= LANES or at + GRID <= 0:
                continue
            piece = r.col[y * XR : (y + 1) * XR, :]
            if at % LANES:
                piece = pltpu.roll(piece, at % LANES, 1)
            keep = (lane >= at) & (lane < at + GRID)
            value = jnp.where(keep, piece, value)
        r.wide[:, t * LANES : (t + 1) * LANES] = value


def inverse_x(r, info, scale):
    for s in range(8):
        r.own[s, TAIL + TILES : ROWS, :] = jnp.zeros((ROWS - TAIL - TILES, LANES), F32)
    for t in range(0, TILES, 4):
        last = min(t + 4, TILES)
        cols = slice(t * LANES, last * LANES)
        pot = -left_dot(r.ix[...], r.wide[:, cols])
        for u in range(t, last):
            part = pot[:, (u - t) * LANES : (u - t + 1) * LANES]
            rows = slice(8 * u, 8 * u + 8)
            one = slice(u * LANES, (u + 1) * LANES)
            tail = part[64:72] * r.blk_tail[:, one]
            for s in range(8):
                piece = part[8 * s : 8 * s + 8]
                r.own[s, rows, :] = piece * r.blk[s, rows, :]
                r.own[s, TAIL + u : TAIL + u + 1, :] = tail[s : s + 1]
                r.wide[8 * s : 8 * s + 8, one] = piece * r.orb[s, rows, :]
            r.wide[64:72, one] = part[64:72] * r.orb_tail[:, one]
    r.wide[:, TILES * LANES :] = jnp.zeros((XR, 2 * LANES), F32)


def share_out(r, info, scale):
    lane = lax.broadcasted_iota(jnp.int32, (GRID, LANES), 1)
    third = lane[:8]

    def turned(tile, turn):
        value = r.wide[:GRID, tile * LANES : (tile + 1) * LANES]
        return pltpu.roll(value, turn, 1) if turn else value

    for band in range(BAND):
        z, x, c = band // 8, band // 2 % 4, band % 2
        core = lax.rem(c + info[MY_C], 2)
        place = 4 * core + lax.rem(x + 4 - info[MY_X], 4)
        z = lax.rem(z + 4 - info[MY_Z], 4)
        t, off = divmod(band * SHARE, LANES)
        turn = (LANES - off) % LANES
        first, second = turned(t, turn), turned(t + 1, turn)
        head, rest = jnp.where(lane < LANES - off, first, second), second
        if off + REST > LANES:
            rest = jnp.where(lane < LANES - off, second, turned(t + 2, turn))
        r.cut[place, z, :GRID, :] = head
        for j in range(3):
            one, two, three = (rest[8 * (3 * j + k) : 8 * (3 * j + k) + 8] for k in range(3))
            two, three = pltpu.roll(two, REST, 1), pltpu.roll(three, 2 * REST, 1)
            packed = jnp.where(third < REST, one, jnp.where(third < 2 * REST, two, three))
            r.cut[place, z, GRID + 8 * j : GRID + 8 * j + 8, :] = packed
    for x in range(4):
        r.keep[x][...] = r.cut[x]
        r.give[x][...] = r.cut[4 + x]


STAGES = (
    whole,
    density,
    forward_x,
    to_columns,
    forward_z,
    along_y,
    inverse_z,
    from_columns,
    inverse_x,
    share_out,
)


def field_kernel(scale, info, *refs):
    tables = ("fx", "ix", "zt", "fy", "iy", "sq")
    scratch = ("orb", "blk", "wide", "orb_tail", "blk_tail", "col", "re", "im", "cut")
    r = types.SimpleNamespace(slabs=refs[:4], mine=refs[4:8], other=refs[8:12])
    vars(r).update(zip(tables, refs[12:18]))
    r.own, r.keep, r.give = refs[18], refs[19:23], refs[23:27]
    vars(r).update(zip(scratch, refs[27:]))
    for stage in STAGES:
        stage(r, info, scale)


def fields(slabs, pieces, scale):
    def body(*refs):
        field_kernel(scale, *refs)

    whole_slabs = pltpu.VMEM((8, ROWS, LANES), F32)
    return call(
        body,
        [shape(8, ROWS, LANES)] + [shape(4, PACK, LANES)] * 8,
        None,
        *slabs,
        *pieces,
        *[jnp.asarray(t) for t in tables()],
        scratch=[
            whole_slabs,
            whole_slabs,
            pltpu.VMEM((XR, (TILES + 2) * LANES), F32),
            pltpu.VMEM((8, TILES * LANES), F32),
            pltpu.VMEM((8, TILES * LANES), F32),
            pltpu.VMEM((GRID * XR, LANES), F32),
            pltpu.VMEM((GRID * KX, LANES), F32),
            pltpu.VMEM((GRID * KX, LANES), F32),
            pltpu.VMEM((8, 4, PACK, LANES), F32),
        ],
        flops=10**10,
        vmem=36,
    )


def send_kernel(info, own_ref, after_ref, *outs):
    for d in range(4):
        y = lax.rem(info[MY_Y] + d, 4)
        outs[d][0] = own_ref[2 * y + info[MY_PAIR]]
        outs[d][1] = own_ref[2 * y + 1 - info[MY_PAIR]]


def add_core_kernel(info, *refs):
    for d in range(3):
        refs[6 + d][...] = refs[d][...] + refs[3 + d][...]


def add_x_kernel(info, k_ref, g_ref, r1, r2, r3, *outs):
    for z in range(4):
        outs[z][...] = k_ref[z] + g_ref[z] + r1[z] + r2[z] + r3[z]


def add_z_kernel(info, s_ref, r1, r2, r3, out_ref, sum_ref):
    sum_ref[...] = s_ref[...] + r1[...] + r2[...] + r3[...]
    out_ref[...] = jnp.zeros((8, PART, LANES), F32)

    def rest(tile):
        value = sum_ref[GRID + 8 * (tile // 3) : GRID + 8 * (tile // 3) + 8, :]
        turn = tile % 3 * REST
        return pltpu.roll(value, LANES - turn, 1) if turn else value

    last = rest(8)
    for s in range(8):
        out_ref[s, 0:8, :] = sum_ref[8 * s : 8 * s + 8, :]
        out_ref[s, 8:16, :] = rest(s)
        out_ref[s, 16:17, :] = sum_ref[64 + s : 65 + s, :]
        out_ref[s, 17:18, :] = last[s : s + 1]


def share_kernel(info, part_ref, after_ref, out_ref):
    for b in range(4):
        total = part_ref[2 * b] + part_ref[2 * b + 1]
        at = (b // 2, b % 2)
        out_ref[at[0], at[1], 0:8, :LANES] = total[0:8]
        out_ref[at[0], at[1], 0:8, LANES:SHARE] = total[8:16, :REST]
        out_ref[at[0], at[1], 8:9, :LANES] = total[16:17]
        out_ref[at[0], at[1], 8:9, LANES:SHARE] = total[17:18, :REST]


def add_y_kernel(info, s_ref, r1, r2, r3, stay_ref, cross_ref):
    for j, ref in enumerate((stay_ref, cross_ref)):
        ref[...] = s_ref[j] + r1[j] + r2[j] + r3[j]


def own_kernel(info, stay_ref, got_ref, out_ref):
    for ref, i in ((stay_ref, info[MY_PAIR]), (got_ref, 1 - info[MY_PAIR])):
        for t in range(TILES):
            wide = min(LANES, PLANE - t * LANES)
            cols = slice(t * LANES, t * LANES + wide)
            out_ref[i, 0:8, cols] = ref[8 * t : 8 * t + 8, :wide]
            out_ref[i, 8:9, cols] = ref[TAIL + t : TAIL + t + 1, :wide]


def shift_x(d):
    return [(i, i // 8 * 8 + (i // 2 + d) % 4 * 2 + i % 2) for i in range(BAND)]


def shift_z(d):
    return [(i, (i + 8 * d) % BAND) for i in range(BAND)]


def shift_y(d):
    return [(i, (i + 2 * d) % 8) for i in range(8)]


def other_slab(x):
    return lax.ppermute(x, "grid", [(i, i ^ 1) for i in range(8)])


def other_core(x):
    return lax.ppermute(x, "band", [(i, i ^ 1) for i in range(BAND)])


def on_device(orbitals, block_owner):
    scale = math.sqrt(GRID**3 / (2 * BAND))
    slab = shape(ROWS, LANES)
    stay, cross, *quarters = call(
        pack_kernel,
        [slab, slab] + [shape(2, QUARTER, LANES)] * 4,
        None,
        orbitals,
        scratch=[pltpu.VMEM((2, ROWS, LANES), F32)],
    )
    pair = call(join_kernel, shape(2, ROWS, LANES), None, stay, other_slab(cross))
    slabs = [pair] + [lax.ppermute(pair, "grid", shift_y(d)) for d in (1, 3)]
    slabs.insert(2, lax.ppermute(slabs[1], "grid", shift_y(1)))

    quarters = quarters[:1] + [lax.ppermute(quarters[d], "band", shift_x(d)) for d in (1, 2, 3)]
    half = shape(4, PIECE, LANES)
    keep, give = call(pick_x_kernel, [half, half], block_owner, *quarters)
    mine = call(pick_core_kernel, half, block_owner, keep, other_core(give))
    along = [mine] + [lax.ppermute(mine, "band", shift_z(d)) for d in (1, 2, 3)]
    mine = call(pick_z_kernel, shape(8, PIECE, LANES), block_owner, *along)
    piece = lax.all_to_all(mine, "grid", 0, 0)
    pieces = [piece] + [lax.ppermute(piece, "band", shift_x(d)) for d in (1, 2, 3)]
    pieces = pieces + [other_core(p) for p in pieces]

    own, *shares = fields(slabs, pieces, scale)
    kept, got = shares[:4], [other_core(g) for g in shares[4:]]
    part = shape(4, PACK, LANES)
    added = call(add_core_kernel, [part] * 3, None, *kept[1:], *got[1:])
    moved = [lax.ppermute(added[d - 1], "band", shift_x(d)) for d in (1, 2, 3)]
    sent = call(send_kernel, [shape(2, ROWS, LANES)] * 4, None, own, after=added[:1])
    sent = [sent[0]] + [lax.ppermute(sent[d], "grid", shift_y(d)) for d in (1, 2, 3)]
    sums = call(add_x_kernel, [shape(PACK, LANES)] * 4, None, kept[0], got[0], *moved)
    moved = [lax.ppermute(sums[d], "band", shift_z(d)) for d in (1, 2, 3)]
    slabs = call(
        add_z_kernel,
        shape(8, PART, LANES),
        None,
        sums[0],
        *moved,
        scratch=[pltpu.VMEM((PACK, LANES), F32)],
    )
    stay, cross = call(add_y_kernel, [slab, slab], None, *sent)
    field = call(own_kernel, shape(2, SLAB, PLANE), None, stay, other_slab(cross))
    slabs = lax.all_to_all(slabs, "grid", 0, 0)
    block_field = call(
        share_kernel, shape(2, 2, SLAB, SHARE), None, slabs, after=[field]
    )
    return field, block_field


def solution(mesh):
    return jax.shard_map(
        on_device,
        mesh=mesh,
        in_specs=(P("band", "grid", None), P()),
        out_specs=(P("band", "grid", None), P(None, None, "grid", "band")),
        check_vma=False,
    )
```

```python
import math
import types

import jax
import jax.numpy as jnp
import numpy as np
from jax import lax
from jax.experimental import pallas as pl
from jax.experimental.pallas import tpu as pltpu
from jax.sharding import PartitionSpec as P

GRID = 72
HALF = GRID // 2 + 1
LINES = 72
GROUP = 20
KX = 40
PLANE = GRID * GRID
TILES = 41
LANES = 128
SLAB = 9
TAIL = 8 * TILES
ROWS = 384
XR = 80
BAND = 32
QUARTER = ROWS // 4
PIECE = ROWS // 8
SHARE = PLANE // BAND
REST = SHARE - LANES
PACK = 96
PART = 24
F32 = jnp.float32
BF16 = jnp.bfloat16


def split_np(table):
    high = table.astype(jnp.bfloat16)
    low = (table - high.astype(np.float64)).astype(jnp.bfloat16)
    return high, low


def tables():
    k = np.arange(GRID)
    ang = 2.0 * np.pi / GRID * ((k[:, None] * k[None, :]) % GRID)
    cos, sin = np.cos(ang), np.sin(ang)
    place = np.arange(GRID)
    plane = np.where(place < 64, SLAB * (place // 8) + place % 8, SLAB * (place - 64) + 8)
    forward_x = np.zeros((2 * KX, XR))
    forward_x[:HALF, :GRID] = cos[:HALF][:, plane]
    forward_x[KX : KX + HALF, :GRID] = -sin[:HALF][:, plane]
    weight = np.where((k[:HALF] == 0) | (k[:HALF] == GRID // 2), 1.0, 2.0) / GRID**3
    inverse_x = np.zeros((XR, 2 * KX))
    inverse_x[:GRID, :HALF] = (weight[:, None] * cos[:HALF][:, plane]).T
    inverse_x[:GRID, KX : KX + HALF] = -(weight[:, None] * sin[:HALF][:, plane]).T
    along_z = np.zeros((LANES, 2 * LANES))
    along_z[:GRID, :GRID] = cos
    along_z[:GRID, LANES : LANES + GRID] = sin
    forward_y = np.block([[cos, sin], [-sin, cos]])
    inverse_y = np.block([[cos, -sin], [sin, cos]])

    def left(table):
        high, low = split_np(table)
        return np.concatenate([high, high, low], axis=1)

    z_high, z_low = split_np(along_z)
    z_three = np.concatenate([z_high, z_high, z_low], axis=0)
    fold = np.where(k > GRID // 2, k - GRID, k).astype(np.float64)
    squares = np.ones((GRID, LANES))
    squares[:, :GRID] = fold[:, None] ** 2 + fold[None, :] ** 2
    return (
        left(forward_x),
        left(inverse_x),
        z_three,
        left(forward_y),
        left(inverse_y),
        squares.astype(np.float32),
    )


def split(x):
    high = x.astype(BF16)
    low = (x - high.astype(F32)).astype(BF16)
    return high, low


def left_dot(table, x):
    high, low = split(x)
    return jnp.dot(table, jnp.concatenate([high, low, high], axis=0), preferred_element_type=F32)


def right_dot(x, table):
    high, low = split(x)
    three = jnp.concatenate([high, low, high], axis=1)
    return jnp.dot(three, table, preferred_element_type=F32)


def pick(index, choices):
    tiles = [c.reshape(-1, 8, LANES) for c in choices]
    value = tiles[0]
    for d in range(1, len(tiles)):
        value = jnp.where(index[None] == d, tiles[d], value)
    return value.reshape(choices[0].shape)


def shape(*dims):
    return jax.ShapeDtypeStruct(dims, F32)


def call(kernel, out_shape, *arrays, after=(), scratch=(), flops=0, vmem=8):
    specs = [pl.BlockSpec(memory_space=pltpu.VMEM) for _ in arrays]
    specs += [pl.BlockSpec(memory_space=pl.ANY) for _ in after]
    size = sum(a.size for a in arrays) * 4

    def body(*refs):
        kernel(scalars(), *refs)

    return pl.pallas_call(
        body,
        in_specs=specs,
        out_shape=out_shape,
        scratch_shapes=list(scratch),
        compiler_params=pltpu.CompilerParams(vmem_limit_bytes=vmem * 2**20),
        cost_estimate=pl.CostEstimate(flops=flops, bytes_accessed=2 * size, transcendentals=0),
    )(*arrays, *after)


MY_X, MY_C, MY_Z, MY_Y, MY_PAIR = range(5)


def scalars():
    band, grid = lax.axis_index("band"), lax.axis_index("grid")
    x, c, z = lax.rem(band // 2, 4), lax.rem(band, 2), band // 8
    return [x, c, z, grid // 2, lax.rem(grid, 2)]


def pack_kernel(info, orb_ref, stay_ref, cross_ref, q0, q1, q2, q3, out_ref):
    for o in range(2):
        out_ref[o, TAIL:ROWS, :] = jnp.zeros((ROWS - TAIL, LANES), F32)
        for t in range(TILES):
            wide = min(LANES, PLANE - t * LANES)
            if wide < LANES:
                out_ref[o, 8 * t : 8 * t + 8, :] = jnp.zeros((8, LANES), F32)
            cols = slice(t * LANES, t * LANES + wide)
            out_ref[o, 8 * t : 8 * t + 8, :wide] = orb_ref[o, 0:8, cols]
            out_ref[o, TAIL + t : TAIL + t + 1, :wide] = orb_ref[o, 8:9, cols]
    stay_ref[...] = out_ref[info[MY_PAIR]]
    cross_ref[...] = out_ref[1 - info[MY_PAIR]]
    for d, quarter in enumerate((q0, q1, q2, q3)):
        first = pl.multiple_of(QUARTER * lax.rem(info[MY_X] + d, 4), QUARTER)
        for o in range(2):
            quarter[o] = out_ref[o, pl.ds(first, QUARTER), :]


def join_kernel(info, stay_ref, got_ref, out_ref):
    out_ref[0] = stay_ref[...]
    out_ref[1] = got_ref[...]


def pick_x_kernel(info, owner_ref, q0, q1, q2, q3, keep_ref, give_ref):
    for ref, half in ((keep_ref, info[MY_C]), (give_ref, 1 - info[MY_C])):
        rows = pl.ds(pl.multiple_of(half * PIECE, PIECE), PIECE)
        for step in range(2):
            away = (info[MY_X] - (owner_ref[step] >> 1)) & 3
            for m in range(2):
                choices = [q[m, rows, :] for q in (q0, q1, q2, q3)]
                ref[2 * step + m] = pick(away, choices)


def pick_core_kernel(info, owner_ref, keep_ref, got_ref, out_ref):
    for b in range(4):
        away = (info[MY_C] - owner_ref[b // 2]) & 1
        out_ref[b] = pick(away, [keep_ref[b], got_ref[b]])


def pick_z_kernel(info, owner_ref, z0, z1, z2, z3, out_ref):
    for b in range(4):
        away = (info[MY_Z] - (owner_ref[b // 2] >> 3)) & 3
        value = pick(away, [z[b] for z in (z0, z1, z2, z3)])
        out_ref[2 * b] = value
        out_ref[2 * b + 1] = value


def whole(r, info, scale):
    for d in range(4):
        y = lax.rem(info[MY_Y] + 4 - d, 4)
        r.orb[2 * y + info[MY_PAIR]] = r.slabs[d][0]
        r.orb[2 * y + 1 - info[MY_PAIR]] = r.slabs[d][1]
    for d in range(4):
        quarter = QUARTER * lax.rem(info[MY_X] + 4 - d, 4)
        for ref, half in ((r.mine[d], info[MY_C]), (r.other[d], 1 - info[MY_C])):
            rows = pl.ds(pl.multiple_of(quarter + PIECE * half, PIECE), PIECE)
            for s in range(8):
                r.blk[s, rows, :] = ref[s]


def density(r, info, scale):
    r.wide[GRID:XR, :] = jnp.zeros((XR - GRID, (TILES + 2) * LANES), F32)
    for t in range(TILES):
        cols = slice(t * LANES, (t + 1) * LANES)
        rows = slice(8 * t, 8 * t + 8)
        for s in range(8):
            r.wide[8 * s : 8 * s + 8, cols] = r.orb[s, rows, :] * r.blk[s, rows, :]
            r.orb_tail[s : s + 1, cols] = r.orb[s, TAIL + t : TAIL + t + 1, :]
            r.blk_tail[s : s + 1, cols] = r.blk[s, TAIL + t : TAIL + t + 1, :]
        r.wide[64:72, cols] = r.orb_tail[:, cols] * r.blk_tail[:, cols]


def forward_x(r, info, scale):
    for t in range(0, TILES, 4):
        cols = slice(t * LANES, min(t + 4, TILES) * LANES)
        r.wide[:, cols] = left_dot(r.fx[...], r.wide[:, cols])


def to_columns(r, info, scale):
    lane = lax.broadcasted_iota(jnp.int32, (XR, LANES), 1)
    for y in range(GRID):
        t, off = divmod(y * GRID, LANES)
        value = r.wide[:, t * LANES : (t + 1) * LANES]
        if off:
            value = pltpu.roll(value, LANES - off, 1)
            if off + GRID > LANES:
                after = pltpu.roll(r.wide[:, (t + 1) * LANES : (t + 2) * LANES], LANES - off, 1)
                value = jnp.where(lane < LANES - off, value, after)
        r.col[y * XR : (y + 1) * XR, :] = value


def forward_z(r, info, scale):
    def step(j, carry):
        base = pl.multiple_of(j * LINES * XR, LINES * XR)
        both = right_dot(r.col[pl.ds(base, LINES * XR), :], r.zt[...])
        base = pl.multiple_of(j * LINES * KX, LINES * KX)
        for y in range(LINES):
            real = both[y * XR : y * XR + KX]
            imag = both[y * XR + KX : (y + 1) * XR]
            rows = pl.ds(base + y * KX, KX)
            r.re[rows, :] = real[:, :LANES] + imag[:, LANES:]
            r.im[rows, :] = imag[:, :LANES] - real[:, LANES:]
        return carry

    lax.fori_loop(0, GRID // LINES, step, 0)


def along_y(r, info, scale):
    def step(j, carry):
        strides = [pl.ds(GROUP * j + q, GRID, stride=KX) for q in range(GROUP)]
        lines = [jnp.concatenate([r.re[s, :], r.im[s, :]], axis=0) for s in strides]
        spec = left_dot(r.fy[...], jnp.concatenate(lines, axis=1))
        factors = []
        for q in range(GROUP):
            kx = (GROUP * j + q).astype(F32)
            square = r.sq[...] + kx * kx
            factor = jnp.where(square > 0, scale / jnp.maximum(square, 1.0), 0.0)
            factors.append(jnp.concatenate([factor, factor], axis=0))
        spec = spec * jnp.concatenate(factors, axis=1)
        back = left_dot(r.iy[...], spec)
        for q, s in enumerate(strides):
            cols = slice(q * LANES, (q + 1) * LANES)
            r.re[s, :] = back[:GRID, cols]
            r.im[s, :] = back[GRID:, cols]
        return carry

    lax.fori_loop(0, KX // GROUP, step, 0)


def inverse_z(r, info, scale):
    def step(j, carry):
        base = pl.multiple_of(j * LINES * KX, LINES * KX)
        rows = pl.ds(base, LINES * KX)
        real = right_dot(r.re[rows, :], r.zt[...])
        imag = right_dot(r.im[rows, :], r.zt[...])
        new_re = real[:, :LANES] - imag[:, LANES:]
        new_im = real[:, LANES:] + imag[:, :LANES]
        base = pl.multiple_of(j * LINES * XR, LINES * XR)
        for y in range(LINES):
            r.col[pl.ds(base + y * XR, KX), :] = new_re[y * KX : (y + 1) * KX]
            r.col[pl.ds(base + y * XR + KX, KX), :] = new_im[y * KX : (y + 1) * KX]
        return carry

    lax.fori_loop(0, GRID // LINES, step, 0)


def from_columns(r, info, scale):
    lane = lax.broadcasted_iota(jnp.int32, (XR, LANES), 1)
    for t in range(TILES):
        value = jnp.zeros((XR, LANES), F32)
        for y in range(GRID):
            at = y * GRID - t * LANES
            if at >= LANES or at + GRID <= 0:
                continue
            piece = r.col[y * XR : (y + 1) * XR, :]
            if at % LANES:
                piece = pltpu.roll(piece, at % LANES, 1)
            keep = (lane >= at) & (lane < at + GRID)
            value = jnp.where(keep, piece, value)
        r.wide[:, t * LANES : (t + 1) * LANES] = value


def inverse_x(r, info, scale):
    for s in range(8):
        r.own[s, TAIL + TILES : ROWS, :] = jnp.zeros((ROWS - TAIL - TILES, LANES), F32)
    for t in range(0, TILES, 4):
        last = min(t + 4, TILES)
        cols = slice(t * LANES, last * LANES)
        pot = -left_dot(r.ix[...], r.wide[:, cols])
        for u in range(t, last):
            part = pot[:, (u - t) * LANES : (u - t + 1) * LANES]
            rows = slice(8 * u, 8 * u + 8)
            one = slice(u * LANES, (u + 1) * LANES)
            tail = part[64:72] * r.blk_tail[:, one]
            for s in range(8):
                piece = part[8 * s : 8 * s + 8]
                r.own[s, rows, :] = piece * r.blk[s, rows, :]
                r.own[s, TAIL + u : TAIL + u + 1, :] = tail[s : s + 1]
                r.wide[8 * s : 8 * s + 8, one] = piece * r.orb[s, rows, :]
            r.wide[64:72, one] = part[64:72] * r.orb_tail[:, one]
    r.wide[:, TILES * LANES :] = jnp.zeros((XR, 2 * LANES), F32)


def share_out(r, info, scale):
    lane = lax.broadcasted_iota(jnp.int32, (GRID, LANES), 1)
    third = lane[:8]

    def turned(tile, turn):
        value = r.wide[:GRID, tile * LANES : (tile + 1) * LANES]
        return pltpu.roll(value, turn, 1) if turn else value

    for band in range(BAND):
        z, x, c = band // 8, band // 2 % 4, band % 2
        core = lax.rem(c + info[MY_C], 2)
        place = 4 * core + lax.rem(x + 4 - info[MY_X], 4)
        z = lax.rem(z + 4 - info[MY_Z], 4)
        t, off = divmod(band * SHARE, LANES)
        turn = (LANES - off) % LANES
        first, second = turned(t, turn), turned(t + 1, turn)
        head, rest = jnp.where(lane < LANES - off, first, second), second
        if off + REST > LANES:
            rest = jnp.where(lane < LANES - off, second, turned(t + 2, turn))
        r.cut[place, z, :GRID, :] = head
        for j in range(3):
            one, two, three = (rest[8 * (3 * j + k) : 8 * (3 * j + k) + 8] for k in range(3))
            two, three = pltpu.roll(two, REST, 1), pltpu.roll(three, 2 * REST, 1)
            packed = jnp.where(third < REST, one, jnp.where(third < 2 * REST, two, three))
            r.cut[place, z, GRID + 8 * j : GRID + 8 * j + 8, :] = packed
    for x in range(4):
        r.keep[x][...] = r.cut[x]
        r.give[x][...] = r.cut[4 + x]


STAGES = (
    whole,
    density,
    forward_x,
    to_columns,
    forward_z,
    along_y,
    inverse_z,
    from_columns,
    inverse_x,
    share_out,
)


def field_kernel(scale, info, *refs):
    tables = ("fx", "ix", "zt", "fy", "iy", "sq")
    scratch = ("orb", "blk", "wide", "orb_tail", "blk_tail", "col", "re", "im", "cut")
    r = types.SimpleNamespace(slabs=refs[:4], mine=refs[4:8], other=refs[8:12])
    vars(r).update(zip(tables, refs[12:18]))
    r.own, r.keep, r.give = refs[18], refs[19:23], refs[23:27]
    vars(r).update(zip(scratch, refs[27:]))
    for stage in STAGES:
        stage(r, info, scale)


def fields(slabs, pieces, scale):
    def body(*refs):
        field_kernel(scale, *refs)

    whole_slabs = pltpu.VMEM((8, ROWS, LANES), F32)
    return call(
        body,
        [shape(8, ROWS, LANES)] + [shape(4, PACK, LANES)] * 8,
        *slabs,
        *pieces,
        *[jnp.asarray(t) for t in tables()],
        scratch=[
            whole_slabs,
            whole_slabs,
            pltpu.VMEM((XR, (TILES + 2) * LANES), F32),
            pltpu.VMEM((8, TILES * LANES), F32),
            pltpu.VMEM((8, TILES * LANES), F32),
            pltpu.VMEM((GRID * XR, LANES), F32),
            pltpu.VMEM((GRID * KX, LANES), F32),
            pltpu.VMEM((GRID * KX, LANES), F32),
            pltpu.VMEM((8, 4, PACK, LANES), F32),
        ],
        flops=10**10,
        vmem=36,
    )


def send_kernel(info, own_ref, after_ref, *outs):
    for d in range(4):
        y = lax.rem(info[MY_Y] + d, 4)
        outs[d][0] = own_ref[2 * y + info[MY_PAIR]]
        outs[d][1] = own_ref[2 * y + 1 - info[MY_PAIR]]


def add_core_kernel(info, *refs):
    for d in range(3):
        refs[6 + d][...] = refs[d][...] + refs[3 + d][...]


def add_x_kernel(info, k_ref, g_ref, r1, r2, r3, *outs):
    for z in range(4):
        outs[z][...] = k_ref[z] + g_ref[z] + r1[z] + r2[z] + r3[z]


def add_z_kernel(info, s_ref, r1, r2, r3, out_ref, sum_ref):
    sum_ref[...] = s_ref[...] + r1[...] + r2[...] + r3[...]
    out_ref[...] = jnp.zeros((8, PART, LANES), F32)

    def rest(tile):
        value = sum_ref[GRID + 8 * (tile // 3) : GRID + 8 * (tile // 3) + 8, :]
        turn = tile % 3 * REST
        return pltpu.roll(value, LANES - turn, 1) if turn else value

    last = rest(8)
    for s in range(8):
        out_ref[s, 0:8, :] = sum_ref[8 * s : 8 * s + 8, :]
        out_ref[s, 8:16, :] = rest(s)
        out_ref[s, 16:17, :] = sum_ref[64 + s : 65 + s, :]
        out_ref[s, 17:18, :] = last[s : s + 1]


def share_kernel(info, part_ref, after_ref, out_ref):
    for b in range(4):
        total = part_ref[2 * b] + part_ref[2 * b + 1]
        at = (b // 2, b % 2)
        out_ref[at[0], at[1], 0:8, :LANES] = total[0:8]
        out_ref[at[0], at[1], 0:8, LANES:SHARE] = total[8:16, :REST]
        out_ref[at[0], at[1], 8:9, :LANES] = total[16:17]
        out_ref[at[0], at[1], 8:9, LANES:SHARE] = total[17:18, :REST]


def add_y_kernel(info, s_ref, r1, r2, r3, stay_ref, cross_ref):
    for j, ref in enumerate((stay_ref, cross_ref)):
        ref[...] = s_ref[j] + r1[j] + r2[j] + r3[j]


def own_kernel(info, stay_ref, got_ref, out_ref):
    for ref, i in ((stay_ref, info[MY_PAIR]), (got_ref, 1 - info[MY_PAIR])):
        for t in range(TILES):
            wide = min(LANES, PLANE - t * LANES)
            cols = slice(t * LANES, t * LANES + wide)
            out_ref[i, 0:8, cols] = ref[8 * t : 8 * t + 8, :wide]
            out_ref[i, 8:9, cols] = ref[TAIL + t : TAIL + t + 1, :wide]


def shift_x(d):
    return [(i, i // 8 * 8 + (i // 2 + d) % 4 * 2 + i % 2) for i in range(BAND)]


def shift_z(d):
    return [(i, (i + 8 * d) % BAND) for i in range(BAND)]


def shift_y(d):
    return [(i, (i + 2 * d) % 8) for i in range(8)]


def other_slab(x):
    return lax.ppermute(x, "grid", [(i, i ^ 1) for i in range(8)])


def other_core(x):
    return lax.ppermute(x, "band", [(i, i ^ 1) for i in range(BAND)])


def on_device(orbitals, block_owner):
    scale = math.sqrt(GRID**3 / (2 * BAND))
    owner = jnp.broadcast_to(block_owner[:, None, None], (2, 8, LANES))
    slab = shape(ROWS, LANES)
    stay, cross, *quarters = call(
        pack_kernel,
        [slab, slab] + [shape(2, QUARTER, LANES)] * 4,
        orbitals,
        scratch=[pltpu.VMEM((2, ROWS, LANES), F32)],
    )
    pair = call(join_kernel, shape(2, ROWS, LANES), stay, other_slab(cross))
    slabs = [pair] + [lax.ppermute(pair, "grid", shift_y(d)) for d in (1, 3)]
    slabs.insert(2, lax.ppermute(slabs[1], "grid", shift_y(1)))

    quarters = quarters[:1] + [lax.ppermute(quarters[d], "band", shift_x(d)) for d in (1, 2, 3)]
    half = shape(4, PIECE, LANES)
    keep, give = call(pick_x_kernel, [half, half], owner, *quarters)
    mine = call(pick_core_kernel, half, owner, keep, other_core(give))
    along = [mine] + [lax.ppermute(mine, "band", shift_z(d)) for d in (1, 2, 3)]
    mine = call(pick_z_kernel, shape(8, PIECE, LANES), owner, *along)
    piece = lax.all_to_all(mine, "grid", 0, 0)
    pieces = [piece] + [lax.ppermute(piece, "band", shift_x(d)) for d in (1, 2, 3)]
    pieces = pieces + [other_core(p) for p in pieces]

    own, *shares = fields(slabs, pieces, scale)
    kept, got = shares[:4], [other_core(g) for g in shares[4:]]
    part = shape(4, PACK, LANES)
    added = call(add_core_kernel, [part] * 3, *kept[1:], *got[1:])
    moved = [lax.ppermute(added[d - 1], "band", shift_x(d)) for d in (1, 2, 3)]
    sent = call(send_kernel, [shape(2, ROWS, LANES)] * 4, own, after=added[:1])
    sent = [sent[0]] + [lax.ppermute(sent[d], "grid", shift_y(d)) for d in (1, 2, 3)]
    sums = call(add_x_kernel, [shape(PACK, LANES)] * 4, kept[0], got[0], *moved)
    moved = [lax.ppermute(sums[d], "band", shift_z(d)) for d in (1, 2, 3)]
    slabs = call(
        add_z_kernel,
        shape(8, PART, LANES),
        sums[0],
        *moved,
        scratch=[pltpu.VMEM((PACK, LANES), F32)],
    )
    stay, cross = call(add_y_kernel, [slab, slab], *sent)
    field = call(own_kernel, shape(2, SLAB, PLANE), stay, other_slab(cross))
    slabs = lax.all_to_all(slabs, "grid", 0, 0)
    block_field = call(
        share_kernel, shape(2, 2, SLAB, SHARE), slabs, after=[field]
    )
    return field, block_field


def solution(mesh):
    return jax.shard_map(
        on_device,
        mesh=mesh,
        in_specs=(P("band", "grid", None), P()),
        out_specs=(P("band", "grid", None), P(None, None, "grid", "band")),
        check_vma=False,
    )
```

```python
import math
import types

import jax
import jax.numpy as jnp
import numpy as np
from jax import lax
from jax.experimental import pallas as pl
from jax.experimental.pallas import tpu as pltpu
from jax.sharding import PartitionSpec as P

GRID = 72
HALF = GRID // 2 + 1
LINES = 72
GROUP = 20
KX = 40
PLANE = GRID * GRID
TILES = 41
LANES = 128
SLAB = 9
TAIL = 8 * TILES
ROWS = 384
XR = 80
BAND = 32
QUARTER = ROWS // 4
PIECE = ROWS // 8
SHARE = PLANE // BAND
REST = SHARE - LANES
PACK = 96
PART = 24
F32 = jnp.float32
BF16 = jnp.bfloat16


def split_np(table):
    high = table.astype(jnp.bfloat16)
    low = (table - high.astype(np.float64)).astype(jnp.bfloat16)
    return high, low


def tables():
    k = np.arange(GRID)
    ang = 2.0 * np.pi / GRID * ((k[:, None] * k[None, :]) % GRID)
    cos, sin = np.cos(ang), np.sin(ang)
    place = np.arange(GRID)
    plane = np.where(place < 64, SLAB * (place // 8) + place % 8, SLAB * (place - 64) + 8)
    forward_x = np.zeros((2 * KX, XR))
    forward_x[:HALF, :GRID] = cos[:HALF][:, plane]
    forward_x[KX : KX + HALF, :GRID] = -sin[:HALF][:, plane]
    weight = np.where((k[:HALF] == 0) | (k[:HALF] == GRID // 2), 1.0, 2.0) / GRID**3
    inverse_x = np.zeros((XR, 2 * KX))
    inverse_x[:GRID, :HALF] = (weight[:, None] * cos[:HALF][:, plane]).T
    inverse_x[:GRID, KX : KX + HALF] = -(weight[:, None] * sin[:HALF][:, plane]).T
    along_z = np.zeros((LANES, 2 * LANES))
    along_z[:GRID, :GRID] = cos
    along_z[:GRID, LANES : LANES + GRID] = sin
    forward_y = np.block([[cos, sin], [-sin, cos]])
    inverse_y = np.block([[cos, -sin], [sin, cos]])

    def left(table):
        high, low = split_np(table)
        return np.concatenate([high, high, low], axis=1)

    z_high, z_low = split_np(along_z)
    z_three = np.concatenate([z_high, z_high, z_low], axis=0)
    fold = np.where(k > GRID // 2, k - GRID, k).astype(np.float64)
    squares = np.ones((GRID, LANES))
    squares[:, :GRID] = fold[:, None] ** 2 + fold[None, :] ** 2
    return (
        left(forward_x),
        left(inverse_x),
        z_three,
        left(forward_y),
        left(inverse_y),
        squares.astype(np.float32),
    )


def split(x):
    high = x.astype(BF16)
    low = (x - high.astype(F32)).astype(BF16)
    return high, low


def left_dot(table, x):
    high, low = split(x)
    return jnp.dot(table, jnp.concatenate([high, low, high], axis=0), preferred_element_type=F32)


def right_dot(x, table):
    high, low = split(x)
    three = jnp.concatenate([high, low, high], axis=1)
    return jnp.dot(three, table, preferred_element_type=F32)


def pick(index, choices):
    tiles = [c.reshape(-1, 8, LANES) for c in choices]
    value = tiles[0]
    for d in range(1, len(tiles)):
        value = jnp.where(index[None] == d, tiles[d], value)
    return value.reshape(choices[0].shape)


def shape(*dims):
    return jax.ShapeDtypeStruct(dims, F32)


def call(kernel, out_shape, *arrays, after=(), scratch=(), flops=0, vmem=8):
    specs = [pl.BlockSpec(memory_space=pltpu.VMEM) for _ in arrays]
    specs += [pl.BlockSpec(memory_space=pl.ANY) for _ in after]
    size = sum(a.size for a in arrays) * 4

    def body(*refs):
        kernel(scalars(), *refs)

    return pl.pallas_call(
        body,
        in_specs=specs,
        out_shape=out_shape,
        scratch_shapes=list(scratch),
        compiler_params=pltpu.CompilerParams(vmem_limit_bytes=vmem * 2**20),
        cost_estimate=pl.CostEstimate(
            flops=flops, bytes_accessed=2 * size if flops else 0, transcendentals=0
        ),
    )(*arrays, *after)


MY_X, MY_C, MY_Z, MY_Y, MY_PAIR = range(5)


def scalars():
    band, grid = lax.axis_index("band"), lax.axis_index("grid")
    x, c, z = lax.rem(band // 2, 4), lax.rem(band, 2), band // 8
    return [x, c, z, grid // 2, lax.rem(grid, 2)]


def pack_kernel(info, orb_ref, stay_ref, cross_ref, q0, q1, q2, q3, out_ref):
    for o in range(2):
        out_ref[o, TAIL:ROWS, :] = jnp.zeros((ROWS - TAIL, LANES), F32)
        for t in range(TILES):
            wide = min(LANES, PLANE - t * LANES)
            if wide < LANES:
                out_ref[o, 8 * t : 8 * t + 8, :] = jnp.zeros((8, LANES), F32)
            cols = slice(t * LANES, t * LANES + wide)
            out_ref[o, 8 * t : 8 * t + 8, :wide] = orb_ref[o, 0:8, cols]
            out_ref[o, TAIL + t : TAIL + t + 1, :wide] = orb_ref[o, 8:9, cols]
    stay_ref[...] = out_ref[info[MY_PAIR]]
    cross_ref[...] = out_ref[1 - info[MY_PAIR]]
    for d, quarter in enumerate((q0, q1, q2, q3)):
        first = pl.multiple_of(QUARTER * lax.rem(info[MY_X] + d, 4), QUARTER)
        for o in range(2):
            quarter[o] = out_ref[o, pl.ds(first, QUARTER), :]


def join_kernel(info, stay_ref, got_ref, out_ref):
    out_ref[0] = stay_ref[...]
    out_ref[1] = got_ref[...]


def pick_x_kernel(info, owner_ref, q0, q1, q2, q3, keep_ref, give_ref):
    for ref, half in ((keep_ref, info[MY_C]), (give_ref, 1 - info[MY_C])):
        rows = pl.ds(pl.multiple_of(half * PIECE, PIECE), PIECE)
        for step in range(2):
            away = (info[MY_X] - (owner_ref[step] >> 1)) & 3
            for m in range(2):
                choices = [q[m, rows, :] for q in (q0, q1, q2, q3)]
                ref[2 * step + m] = pick(away, choices)


def pick_core_kernel(info, owner_ref, keep_ref, got_ref, out_ref):
    for b in range(4):
        away = (info[MY_C] - owner_ref[b // 2]) & 1
        out_ref[b] = pick(away, [keep_ref[b], got_ref[b]])


def pick_z_kernel(info, owner_ref, z0, z1, z2, z3, out_ref):
    for b in range(4):
        away = (info[MY_Z] - (owner_ref[b // 2] >> 3)) & 3
        value = pick(away, [z[b] for z in (z0, z1, z2, z3)])
        out_ref[2 * b] = value
        out_ref[2 * b + 1] = value


def whole(r, info, scale):
    for d in range(4):
        y = lax.rem(info[MY_Y] + 4 - d, 4)
        r.orb[2 * y + info[MY_PAIR]] = r.slabs[d][0]
        r.orb[2 * y + 1 - info[MY_PAIR]] = r.slabs[d][1]
    for d in range(4):
        quarter = QUARTER * lax.rem(info[MY_X] + 4 - d, 4)
        for ref, half in ((r.mine[d], info[MY_C]), (r.other[d], 1 - info[MY_C])):
            rows = pl.ds(pl.multiple_of(quarter + PIECE * half, PIECE), PIECE)
            for s in range(8):
                r.blk[s, rows, :] = ref[s]


def density(r, info, scale):
    r.wide[GRID:XR, :] = jnp.zeros((XR - GRID, (TILES + 2) * LANES), F32)
    for t in range(TILES):
        cols = slice(t * LANES, (t + 1) * LANES)
        rows = slice(8 * t, 8 * t + 8)
        for s in range(8):
            r.wide[8 * s : 8 * s + 8, cols] = r.orb[s, rows, :] * r.blk[s, rows, :]
            r.orb_tail[s : s + 1, cols] = r.orb[s, TAIL + t : TAIL + t + 1, :]
            r.blk_tail[s : s + 1, cols] = r.blk[s, TAIL + t : TAIL + t + 1, :]
        r.wide[64:72, cols] = r.orb_tail[:, cols] * r.blk_tail[:, cols]


def forward_x(r, info, scale):
    for t in range(0, TILES, 4):
        cols = slice(t * LANES, min(t + 4, TILES) * LANES)
        r.wide[:, cols] = left_dot(r.fx[...], r.wide[:, cols])


def to_columns(r, info, scale):
    lane = lax.broadcasted_iota(jnp.int32, (XR, LANES), 1)
    for y in range(GRID):
        t, off = divmod(y * GRID, LANES)
        value = r.wide[:, t * LANES : (t + 1) * LANES]
        if off:
            value = pltpu.roll(value, LANES - off, 1)
            if off + GRID > LANES:
                after = pltpu.roll(r.wide[:, (t + 1) * LANES : (t + 2) * LANES], LANES - off, 1)
                value = jnp.where(lane < LANES - off, value, after)
        r.col[y * XR : (y + 1) * XR, :] = value


def forward_z(r, info, scale):
    def step(j, carry):
        base = pl.multiple_of(j * LINES * XR, LINES * XR)
        both = right_dot(r.col[pl.ds(base, LINES * XR), :], r.zt[...])
        base = pl.multiple_of(j * LINES * KX, LINES * KX)
        for y in range(LINES):
            real = both[y * XR : y * XR + KX]
            imag = both[y * XR + KX : (y + 1) * XR]
            rows = pl.ds(base + y * KX, KX)
            r.re[rows, :] = real[:, :LANES] + imag[:, LANES:]
            r.im[rows, :] = imag[:, :LANES] - real[:, LANES:]
        return carry

    lax.fori_loop(0, GRID // LINES, step, 0)


def along_y(r, info, scale):
    def step(j, carry):
        strides = [pl.ds(GROUP * j + q, GRID, stride=KX) for q in range(GROUP)]
        lines = [jnp.concatenate([r.re[s, :], r.im[s, :]], axis=0) for s in strides]
        spec = left_dot(r.fy[...], jnp.concatenate(lines, axis=1))
        factors = []
        for q in range(GROUP):
            kx = (GROUP * j + q).astype(F32)
            square = r.sq[...] + kx * kx
            factor = jnp.where(square > 0, scale / jnp.maximum(square, 1.0), 0.0)
            factors.append(jnp.concatenate([factor, factor], axis=0))
        spec = spec * jnp.concatenate(factors, axis=1)
        back = left_dot(r.iy[...], spec)
        for q, s in enumerate(strides):
            cols = slice(q * LANES, (q + 1) * LANES)
            r.re[s, :] = back[:GRID, cols]
            r.im[s, :] = back[GRID:, cols]
        return carry

    lax.fori_loop(0, KX // GROUP, step, 0)


def inverse_z(r, info, scale):
    def step(j, carry):
        base = pl.multiple_of(j * LINES * KX, LINES * KX)
        rows = pl.ds(base, LINES * KX)
        real = right_dot(r.re[rows, :], r.zt[...])
        imag = right_dot(r.im[rows, :], r.zt[...])
        new_re = real[:, :LANES] - imag[:, LANES:]
        new_im = real[:, LANES:] + imag[:, :LANES]
        base = pl.multiple_of(j * LINES * XR, LINES * XR)
        for y in range(LINES):
            r.col[pl.ds(base + y * XR, KX), :] = new_re[y * KX : (y + 1) * KX]
            r.col[pl.ds(base + y * XR + KX, KX), :] = new_im[y * KX : (y + 1) * KX]
        return carry

    lax.fori_loop(0, GRID // LINES, step, 0)


def from_columns(r, info, scale):
    lane = lax.broadcasted_iota(jnp.int32, (XR, LANES), 1)
    for t in range(TILES):
        value = jnp.zeros((XR, LANES), F32)
        for y in range(GRID):
            at = y * GRID - t * LANES
            if at >= LANES or at + GRID <= 0:
                continue
            piece = r.col[y * XR : (y + 1) * XR, :]
            if at % LANES:
                piece = pltpu.roll(piece, at % LANES, 1)
            keep = (lane >= at) & (lane < at + GRID)
            value = jnp.where(keep, piece, value)
        r.wide[:, t * LANES : (t + 1) * LANES] = value


def inverse_x(r, info, scale):
    for s in range(8):
        r.own[s, TAIL + TILES : ROWS, :] = jnp.zeros((ROWS - TAIL - TILES, LANES), F32)
    for t in range(0, TILES, 4):
        last = min(t + 4, TILES)
        cols = slice(t * LANES, last * LANES)
        pot = -left_dot(r.ix[...], r.wide[:, cols])
        for u in range(t, last):
            part = pot[:, (u - t) * LANES : (u - t + 1) * LANES]
            rows = slice(8 * u, 8 * u + 8)
            one = slice(u * LANES, (u + 1) * LANES)
            tail = part[64:72] * r.blk_tail[:, one]
            for s in range(8):
                piece = part[8 * s : 8 * s + 8]
                r.own[s, rows, :] = piece * r.blk[s, rows, :]
                r.own[s, TAIL + u : TAIL + u + 1, :] = tail[s : s + 1]
                r.wide[8 * s : 8 * s + 8, one] = piece * r.orb[s, rows, :]
            r.wide[64:72, one] = part[64:72] * r.orb_tail[:, one]
    r.wide[:, TILES * LANES :] = jnp.zeros((XR, 2 * LANES), F32)


def share_out(r, info, scale):
    lane = lax.broadcasted_iota(jnp.int32, (GRID, LANES), 1)
    third = lane[:8]

    def turned(tile, turn):
        value = r.wide[:GRID, tile * LANES : (tile + 1) * LANES]
        return pltpu.roll(value, turn, 1) if turn else value

    for band in range(BAND):
        z, x, c = band // 8, band // 2 % 4, band % 2
        core = lax.rem(c + info[MY_C], 2)
        place = 4 * core + lax.rem(x + 4 - info[MY_X], 4)
        z = lax.rem(z + 4 - info[MY_Z], 4)
        t, off = divmod(band * SHARE, LANES)
        turn = (LANES - off) % LANES
        first, second = turned(t, turn), turned(t + 1, turn)
        head, rest = jnp.where(lane < LANES - off, first, second), second
        if off + REST > LANES:
            rest = jnp.where(lane < LANES - off, second, turned(t + 2, turn))
        r.cut[place, z, :GRID, :] = head
        for j in range(3):
            one, two, three = (rest[8 * (3 * j + k) : 8 * (3 * j + k) + 8] for k in range(3))
            two, three = pltpu.roll(two, REST, 1), pltpu.roll(three, 2 * REST, 1)
            packed = jnp.where(third < REST, one, jnp.where(third < 2 * REST, two, three))
            r.cut[place, z, GRID + 8 * j : GRID + 8 * j + 8, :] = packed
    for x in range(4):
        r.keep[x][...] = r.cut[x]
        r.give[x][...] = r.cut[4 + x]


STAGES = (
    whole,
    density,
    forward_x,
    to_columns,
    forward_z,
    along_y,
    inverse_z,
    from_columns,
    inverse_x,
    share_out,
)


def field_kernel(scale, info, *refs):
    tables = ("fx", "ix", "zt", "fy", "iy", "sq")
    scratch = ("orb", "blk", "wide", "orb_tail", "blk_tail", "col", "re", "im", "cut")
    r = types.SimpleNamespace(slabs=refs[:4], mine=refs[4:8], other=refs[8:12])
    vars(r).update(zip(tables, refs[12:18]))
    r.own, r.keep, r.give = refs[18], refs[19:23], refs[23:27]
    vars(r).update(zip(scratch, refs[27:]))
    for stage in STAGES:
        stage(r, info, scale)


def fields(slabs, pieces, scale):
    def body(*refs):
        field_kernel(scale, *refs)

    whole_slabs = pltpu.VMEM((8, ROWS, LANES), F32)
    return call(
        body,
        [shape(8, ROWS, LANES)] + [shape(4, PACK, LANES)] * 8,
        *slabs,
        *pieces,
        *[jnp.asarray(t) for t in tables()],
        scratch=[
            whole_slabs,
            whole_slabs,
            pltpu.VMEM((XR, (TILES + 2) * LANES), F32),
            pltpu.VMEM((8, TILES * LANES), F32),
            pltpu.VMEM((8, TILES * LANES), F32),
            pltpu.VMEM((GRID * XR, LANES), F32),
            pltpu.VMEM((GRID * KX, LANES), F32),
            pltpu.VMEM((GRID * KX, LANES), F32),
            pltpu.VMEM((8, 4, PACK, LANES), F32),
        ],
        flops=10**10,
        vmem=36,
    )


def send_kernel(info, own_ref, after_ref, *outs):
    for d in range(4):
        y = lax.rem(info[MY_Y] + d, 4)
        outs[d][0] = own_ref[2 * y + info[MY_PAIR]]
        outs[d][1] = own_ref[2 * y + 1 - info[MY_PAIR]]


def add_core_kernel(info, *refs):
    for d in range(3):
        refs[6 + d][...] = refs[d][...] + refs[3 + d][...]


def add_x_kernel(info, k_ref, g_ref, r1, r2, r3, *outs):
    for z in range(4):
        outs[z][...] = k_ref[z] + g_ref[z] + r1[z] + r2[z] + r3[z]


def add_z_kernel(info, s_ref, r1, r2, r3, out_ref, sum_ref):
    sum_ref[...] = s_ref[...] + r1[...] + r2[...] + r3[...]
    out_ref[...] = jnp.zeros((8, PART, LANES), F32)

    def rest(tile):
        value = sum_ref[GRID + 8 * (tile // 3) : GRID + 8 * (tile // 3) + 8, :]
        turn = tile % 3 * REST
        return pltpu.roll(value, LANES - turn, 1) if turn else value

    last = rest(8)
    for s in range(8):
        out_ref[s, 0:8, :] = sum_ref[8 * s : 8 * s + 8, :]
        out_ref[s, 8:16, :] = rest(s)
        out_ref[s, 16:17, :] = sum_ref[64 + s : 65 + s, :]
        out_ref[s, 17:18, :] = last[s : s + 1]


def share_kernel(info, part_ref, after_ref, out_ref):
    for b in range(4):
        total = part_ref[2 * b] + part_ref[2 * b + 1]
        at = (b // 2, b % 2)
        out_ref[at[0], at[1], 0:8, :LANES] = total[0:8]
        out_ref[at[0], at[1], 0:8, LANES:SHARE] = total[8:16, :REST]
        out_ref[at[0], at[1], 8:9, :LANES] = total[16:17]
        out_ref[at[0], at[1], 8:9, LANES:SHARE] = total[17:18, :REST]


def add_y_kernel(info, s_ref, r1, r2, r3, stay_ref, cross_ref):
    for j, ref in enumerate((stay_ref, cross_ref)):
        ref[...] = s_ref[j] + r1[j] + r2[j] + r3[j]


def own_kernel(info, stay_ref, got_ref, out_ref):
    for ref, i in ((stay_ref, info[MY_PAIR]), (got_ref, 1 - info[MY_PAIR])):
        for t in range(TILES):
            wide = min(LANES, PLANE - t * LANES)
            cols = slice(t * LANES, t * LANES + wide)
            out_ref[i, 0:8, cols] = ref[8 * t : 8 * t + 8, :wide]
            out_ref[i, 8:9, cols] = ref[TAIL + t : TAIL + t + 1, :wide]


def shift_x(d):
    return [(i, i // 8 * 8 + (i // 2 + d) % 4 * 2 + i % 2) for i in range(BAND)]


def shift_z(d):
    return [(i, (i + 8 * d) % BAND) for i in range(BAND)]


def shift_y(d):
    return [(i, (i + 2 * d) % 8) for i in range(8)]


def other_slab(x):
    return lax.ppermute(x, "grid", [(i, i ^ 1) for i in range(8)])


def other_core(x):
    return lax.ppermute(x, "band", [(i, i ^ 1) for i in range(BAND)])


def on_device(orbitals, block_owner):
    scale = math.sqrt(GRID**3 / (2 * BAND))
    owner = jnp.broadcast_to(block_owner[:, None, None], (2, 8, LANES))
    slab = shape(ROWS, LANES)
    stay, cross, *quarters = call(
        pack_kernel,
        [slab, slab] + [shape(2, QUARTER, LANES)] * 4,
        orbitals,
        scratch=[pltpu.VMEM((2, ROWS, LANES), F32)],
    )
    pair = call(join_kernel, shape(2, ROWS, LANES), stay, other_slab(cross))
    slabs = [pair] + [lax.ppermute(pair, "grid", shift_y(d)) for d in (1, 3)]
    slabs.insert(2, lax.ppermute(slabs[1], "grid", shift_y(1)))

    quarters = quarters[:1] + [lax.ppermute(quarters[d], "band", shift_x(d)) for d in (1, 2, 3)]
    half = shape(4, PIECE, LANES)
    keep, give = call(pick_x_kernel, [half, half], owner, *quarters)
    mine = call(pick_core_kernel, half, owner, keep, other_core(give))
    along = [mine] + [lax.ppermute(mine, "band", shift_z(d)) for d in (1, 2, 3)]
    mine = call(pick_z_kernel, shape(8, PIECE, LANES), owner, *along)
    piece = lax.all_to_all(mine, "grid", 0, 0)
    pieces = [piece] + [lax.ppermute(piece, "band", shift_x(d)) for d in (1, 2, 3)]
    pieces = pieces + [other_core(p) for p in pieces]

    own, *shares = fields(slabs, pieces, scale)
    kept, got = shares[:4], [other_core(g) for g in shares[4:]]
    part = shape(4, PACK, LANES)
    added = call(add_core_kernel, [part] * 3, *kept[1:], *got[1:])
    moved = [lax.ppermute(added[d - 1], "band", shift_x(d)) for d in (1, 2, 3)]
    sent = call(send_kernel, [shape(2, ROWS, LANES)] * 4, own, after=added[:1])
    sent = [sent[0]] + [lax.ppermute(sent[d], "grid", shift_y(d)) for d in (1, 2, 3)]
    sums = call(add_x_kernel, [shape(PACK, LANES)] * 4, kept[0], got[0], *moved)
    moved = [lax.ppermute(sums[d], "band", shift_z(d)) for d in (1, 2, 3)]
    slabs = call(
        add_z_kernel,
        shape(8, PART, LANES),
        sums[0],
        *moved,
        scratch=[pltpu.VMEM((PACK, LANES), F32)],
    )
    stay, cross = call(add_y_kernel, [slab, slab], *sent)
    field = call(own_kernel, shape(2, SLAB, PLANE), stay, other_slab(cross))
    slabs = lax.all_to_all(slabs, "grid", 0, 0)
    block_field = call(
        share_kernel, shape(2, 2, SLAB, SHARE), slabs, after=[field]
    )
    return field, block_field


def solution(mesh):
    return jax.shard_map(
        on_device,
        mesh=mesh,
        in_specs=(P("band", "grid", None), P()),
        out_specs=(P("band", "grid", None), P(None, None, "grid", "band")),
        check_vma=False,
    )
```
